128 devices in a mesh: sec: 8 (over z_hi, y), op: 16 (over x, z_lo, core).
Axes of the slice: x: 4, y: 4, z: 4 (z_hi: 2, z_lo: 2; z = z_hi * 2 + z_lo), core: 2. Of those that a mesh axis runs over, the one named last changes fastest.
Arguments:
- state: float32 [8, 1024, 1024], P('sec'), may hold values from -6 to 6
- left_ops: float32 [16, 8, 1024, 1024], P('op', 'sec'), may hold values from -1 to 1
- right_ops: float32 [16, 8, 1024, 1024], P('op', 'sec'), may hold values from -1 to 1
- charge: int32 [16], P('op'), may hold values from -1 to 1, as said below
- sizes: int32 [8], P('sec'), may hold values from 64 to 1024, as said below
Outputs:
- next_vector: float32 [8, 1024, 1024], P('sec', 'op')
- next_sigma: float32 [8, 1024, 1024], P('sec', 'op')
- projected: float32 [2], replicated
The draws below stay inside these ranges and needn't reach their ends.
Inputs may be any that keep to these rules, and one draw needn't show every extreme that they name: Each of -1, 0 and 1 is the charge of some operator. `sizes`: some sector holds exactly 1024 states and another exactly 64.
All inputs are finite; a program needn't handle non-finite values.
Results may differ from the reference program's by a relative error of at most 0.0003.
Values sent between devices are 32-bit elements; how exact they have to be, the bound alone decides.
A program may use at most 128 MiB of HBM per device.

```python
import math
import jax
import jax.numpy as jnp
from jax import lax

BLK = 1024
SECT = 8
OPS = 16


def draw_charge(key, part):
    ordering = jax.random.permutation(jax.random.fold_in(key, 11), OPS)
    return (ordering % 3 - 1).astype(jnp.int32)


def draw_sizes(key, part):
    first_key = jax.random.fold_in(key, 21)
    second_key = jax.random.fold_in(key, 22)
    third_key = jax.random.fold_in(key, 23)
    drawn = jax.random.randint(first_key, (SECT,), BLK // 16, BLK + 1)
    largest_at = jax.random.randint(second_key, (), 0, SECT)
    smallest_at = (largest_at + 1 + jax.random.randint(third_key, (), 0, SECT - 1)) % SECT
    position = jnp.arange(SECT, dtype=jnp.int32)
    drawn = jnp.where(position == largest_at, BLK, drawn)
    drawn = jnp.where(position == smallest_at, BLK // 16, drawn)
    return drawn.astype(jnp.int32)


def with_diagonal(noise, diagonal_value, noise_scale):
    identity = (jnp.arange(BLK, dtype=jnp.int32)[:, None] == jnp.arange(BLK, dtype=jnp.int32)[None, :]).astype(jnp.float32)
    return diagonal_value * identity + noise * (noise_scale / math.sqrt(BLK))


def draw_left_ops(key, part):
    key = jax.random.fold_in(key, 31)
    noise = jnp.clip(jax.random.normal(key, (OPS, SECT, BLK, BLK), jnp.float32), -2.0, 2.0)
    return with_diagonal(noise, 0.5, 0.5)


def draw_right_ops(key, part):
    key = jax.random.fold_in(key, 32)
    noise = jnp.clip(jax.random.normal(key, (OPS, SECT, BLK, BLK), jnp.float32), -2.0, 2.0)
    return with_diagonal(noise, 0.5, 0.5)


def shard_levels(own_key, extent, split, least, high):
    factor_of = 1.0
    for axis_at, blocks in split:
        steps = jax.random.uniform(jax.random.fold_in(jax.random.fold_in(own_key, 6), axis_at), (blocks,), jnp.float32, least / len(split), high / len(split))
        factor_of = factor_of * jnp.repeat(jnp.exp(steps), extent[axis_at] // blocks).reshape((-1,) + (1,) * (len(extent) - 1 - axis_at))
    return factor_of


def bell_draw(rng, extent, deviation, bound, shards=(), kind=jnp.bfloat16):
    factor_of = shard_levels(rng, extent, shards, -0.22, 0.18) if shards else 1.0
    values = jax.random.normal(rng, extent, jnp.float32) * deviation * factor_of
    return jnp.minimum(jnp.maximum(values, -bound), bound).astype(kind)


def setup_inputs(seed: int = 0) -> dict:
    key_of = jax.random.split(jax.random.key(seed), 6)
    return {
        "state": bell_draw(key_of[0], (SECT, BLK, BLK), 1.0, 6.0, ((0, 8),), jnp.float32),
        "left_ops": draw_left_ops(jax.random.fold_in(key_of[5], 71), 0),
        "right_ops": draw_right_ops(jax.random.fold_in(key_of[5], 71), 0),
        "charge": draw_charge(jax.random.fold_in(key_of[5], 71), 0),
        "sizes": draw_sizes(jax.random.fold_in(key_of[5], 71), 0),
    }


epsilon = 1e-06

def block_mask(sizes):
    alive = (jnp.arange(BLK, dtype=jnp.int32)[None, :] < sizes[:, None]).astype(jnp.float32)
    return alive[:, :, None] * alive[:, None, :]

def sigma(vector, left_ops, right_ops, charge, live_mask):
    blank = jnp.zeros((1, BLK, BLK), jnp.float32)

    def step(total, item):
        left_blocks, right_blocks, charge_now = item
        moved = jnp.einsum('sij,sjl->sil', left_blocks, vector, precision=lax.Precision.HIGHEST)
        padded = jnp.concatenate([blank.astype(moved.dtype), moved, blank.astype(moved.dtype)], axis=0)
        shifted = lax.dynamic_slice_in_dim(padded, (1 - charge_now).astype(jnp.int32), SECT, 0)
        product = jnp.einsum('til,tml->tim', shifted, right_blocks, precision=lax.Precision.HIGHEST)
        return (total + product, None)
    total, unused = lax.scan(step, jnp.zeros_like(vector), (left_ops, right_ops, charge))
    return total * live_mask

def reference(state, left_ops, right_ops, charge, sizes):
    live_mask = block_mask(sizes)
    cell_count = 1.0 * SECT * BLK * BLK
    start = state * live_mask
    first_vector = start * lax.rsqrt(jnp.sum(start * start) / cell_count + epsilon)
    first_sigma = sigma(first_vector, left_ops, right_ops, charge, live_mask)
    rayleigh_one = jnp.sum(first_vector * first_sigma) / cell_count
    residual = first_sigma - rayleigh_one * first_vector
    next_vector = residual * lax.rsqrt(jnp.sum(residual * residual) / cell_count + epsilon)
    next_sigma = sigma(next_vector, left_ops, right_ops, charge, live_mask)
    rayleigh_two = jnp.sum(next_vector * next_sigma) / cell_count
    return (next_vector, next_sigma, jnp.stack([rayleigh_one, rayleigh_two]))
```

```python
import functools
import jax
import jax.numpy as jnp
from jax import lax
from jax.experimental import pallas as pl
from jax.experimental.pallas import tpu as pltpu
from jax.sharding import PartitionSpec as P

epsilon = 1e-06
CHUNKS = 4
F32 = jnp.float32
BF16 = jnp.bfloat16
MESH = pl.DeviceIdType.MESH


def split(x):
    high = x.astype(BF16)
    return high, (x - high.astype(F32)).astype(BF16)


def dot3(a_high, a_low, b_high, b_low, contract):
    def one(a, b):
        return lax.dot_general(a, b, (contract, ((), ())), preferred_element_type=F32)
    return one(a_high, b_high) + (one(a_high, b_low) + one(a_low, b_high))


def kernel(
    nq, ns, state_ref, l_ref, r_ref, charge_ref, sizes_ref,
    nv_ref, out_sigma_ref, proj_ref,
    l_high, l_low, v_high, v_low, p_high, p_low, x_own, x_sent, x_got,
    y_out, y_got, t_out, t_got, sig, gathered, klass, tile_out, op_got, sec_got,
    x_send, x_recv, y_send, y_recv, t_send, t_recv, g_send, g_recv,
    k_send, k_recv, op_send, op_recv, sec_send, sec_recv,
):
    no, share, n = state_ref.shape
    rq, cq = share // nq, n // nq
    s = lax.axis_index("sec")
    k = lax.axis_index("op")
    core = k % 2
    zlo = (k // 2) % 2
    x = k // 4
    nx = no // 4
    d = 1 - 2 * core
    dst, src = s + d, s - d
    has_dst = (dst >= 0) & (dst < ns)
    has_src = (src >= 0) & (src < ns)
    has_up = s < ns - 1
    has_down = s > 0
    charge = charge_ref[0]
    size = sizes_ref[0]
    cells = 1.0 * ns * n * n
    crossed = charge == -d

    barrier = pltpu.get_barrier_semaphore()

    def greet_op(j, carry):
        pl.semaphore_signal(barrier, inc=1, device_id=(s, (k + j) % no), device_id_type=MESH)
        return carry

    def greet_sec(j, carry):
        pl.semaphore_signal(barrier, inc=1, device_id=((s + j) % ns, k), device_id_type=MESH)
        return carry

    lax.fori_loop(1, no, greet_op, 0)
    lax.fori_loop(1, ns, greet_sec, 0)

    def op_copy(source, target, send, recv, j):
        return pltpu.make_async_remote_copy(
            src_ref=source, dst_ref=target.at[j], send_sem=send, recv_sem=recv,
            device_id=(s, (k + j) % no), device_id_type=MESH)

    def sec_copy(source, target, send, recv, j):
        return pltpu.make_async_remote_copy(
            src_ref=source, dst_ref=target.at[j], send_sem=send, recv_sem=recv,
            device_id=((s + j) % ns, k), device_id_type=MESH)

    def wait_many(target, send, recv, count):
        whole = target.at[pl.ds(1, count - 1)]
        copy = pltpu.make_async_remote_copy(
            src_ref=whole, dst_ref=whole, send_sem=send, recv_sem=recv,
            device_id=(s, (k + 1) % no), device_id_type=MESH)
        copy.wait_send()
        copy.wait_recv()

    def op_start(which, value):
        op_got[which, 0] = jnp.full((8, 128), value, F32)

        def body(j, carry):
            op_copy(op_got.at[which, 0], op_got.at[which], op_send.at[which], op_recv.at[which], j).start()
            return carry
        lax.fori_loop(1, no, body, 0)

    def op_finish(which):
        wait_many(op_got.at[which], op_send.at[which], op_recv.at[which], no)
        total = jnp.zeros((8, 128), F32)
        for i in range(no):
            total = total + op_got[which, (k + no - i) % no]
        return total

    def sec_start(which, tile):
        sec_got[which, 0] = tile

        def body(j, carry):
            sec_copy(sec_got.at[which, 0], sec_got.at[which], sec_send.at[which], sec_recv.at[which], j).start()
            return carry
        lax.fori_loop(1, ns, body, 0)

    def sec_finish(which):
        wait_many(sec_got.at[which], sec_send.at[which], sec_recv.at[which], ns)
        total = jnp.zeros((8, 128), F32)
        for i in range(ns):
            total = total + sec_got[which, (s + ns - i) % ns]
        return total

    def shifted(source, q):
        return pltpu.make_async_remote_copy(
            src_ref=source.at[q], dst_ref=x_got.at[q], send_sem=x_send.at[q], recv_sem=x_recv.at[q],
            device_id=((dst + ns) % ns, k), device_id_type=MESH)

    columns = lax.broadcasted_iota(jnp.int32, (share, n), 1) < size
    rows = lax.broadcasted_iota(jnp.int32, (share, n), 0)

    def live(block):
        return columns & (rows + block * share < size)

    def start_block(block):
        return jnp.where(live(block), state_ref[block], 0.0)

    def fill_start(block, total):
        value = start_block(block)
        at = pl.ds(pl.multiple_of(block * share, share), share)
        v_high[at], v_low[at] = split(value)
        return total + jnp.sum((value * value).reshape(share // 8, 8, n), axis=0)

    squares = lax.fori_loop(0, no, fill_start, jnp.zeros((8, n), F32))
    start_square = jnp.sum(squares)

    @pl.when(jnp.logical_not(has_src))
    def _():
        x_got[...] = jnp.zeros_like(x_got)

    @pl.when(jnp.logical_not(has_up))
    def _():
        t_got[0] = jnp.zeros(t_got.shape[1:], F32)

    @pl.when(jnp.logical_not(has_down))
    def _():
        t_got[1] = jnp.zeros(t_got.shape[1:], F32)

    pl.semaphore_wait(barrier, no - 1 + ns - 1)

    klass[0] = jnp.full((8, 128), jnp.where(crossed, charge, 0), jnp.int32).astype(F32)

    def klass_body(j, carry):
        op_copy(klass.at[0], klass, k_send, k_recv, j).start()
        return carry
    lax.fori_loop(1, no, klass_body, 0)
    sec_start(0, jnp.full((8, 128), start_square, F32))

    def left_products(first):
        def body(q, carry):
            if first:
                at = pl.ds(pl.multiple_of(q * rq, rq), rq)
                high, low = split(l_ref[:, at, :].reshape(no * rq, n))
                l_high[q] = high
                l_low[q] = low
            else:
                high, low = l_high[q], l_low[q]
            product = dot3(high, low, v_high[...], v_low[...], ((1,), (0,)))
            x_own[q] = product
            if first:
                right = r_ref[q]
                x_sent[q] = jnp.where(charge == d, product, right)
                p_high[q], p_low[q] = split(jnp.where(crossed, product, right))

            @pl.when(has_dst)
            def _():
                shifted(x_sent if first else x_own, q).start()
            return carry
        lax.fori_loop(0, nq, body, 0)

    def t_copy(way, q):
        to = s - 1 if way == 0 else s + 1
        return pltpu.make_async_remote_copy(
            src_ref=t_out.at[way, q], dst_ref=t_got.at[way, q], send_sem=t_send.at[way, q],
            recv_sem=t_recv.at[way, q], device_id=((to + ns) % ns, k), device_id_type=MESH)

    def weight(j, which):
        w = (klass[j] == which).astype(F32)
        return jnp.concatenate([w] * (cq // 128), axis=1)[None]

    def reduce_chunk(q):
        wait_many(y_got.at[q], y_send.at[q], y_recv.at[q], no)

        def body(j, totals):
            part = y_got[q, j].reshape(share // 8, 8, cq)
            return tuple(t + part * weight(j, w) for t, w in zip(totals, (0.0, -1.0, 1.0)))

        own = y_out[q, k].reshape(share // 8, 8, cq)
        totals = tuple(own * weight(0, w) for w in (0.0, -1.0, 1.0))
        totals = lax.fori_loop(1, no, body, totals)
        here, below, above = (t.reshape(share, cq) for t in totals)
        at = pl.ds(pl.multiple_of(q * rq, rq), rq)
        for p in range(nq):
            sig[at, p * cq:(p + 1) * cq] = here[p * rq:(p + 1) * rq]
        t_out[0, q] = below
        t_out[1, q] = above

        @pl.when(has_down)
        def _():
            t_copy(0, q).start()

        @pl.when(has_up)
        def _():
            t_copy(1, q).start()

    def right_products(first):
        def body(q, carry):
            @pl.when(has_src)
            def _():
                shifted(x_sent, q).wait_recv()
            use_own = charge == 0 if first else charge != d
            high, low = split(jnp.where(use_own, x_own[q], x_got[q]))
            for p in range(nq):
                block = dot3(high, low, p_high[p], p_low[p], ((1,), (1,)))
                if first:
                    block = jnp.where(crossed, block.T, block)
                y_out[q, :, p * rq:(p + 1) * rq, :] = block.reshape(no, rq, cq)

            def send(j, carry):
                to = (k + j) % no
                op_copy(y_out.at[q, to], y_got.at[q], y_send.at[q], y_recv.at[q], j).start()
                return carry
            lax.fori_loop(1, no, send, 0)

            @pl.when(q > 0)
            def _():
                reduce_chunk(q - 1)
            return carry
        lax.fori_loop(0, nq, body, 0)

        @pl.when(has_dst)
        def _():
            def done(q, carry):
                shifted(x_sent if first else x_own, q).wait_send()
                return carry
            lax.fori_loop(0, nq, done, 0)
        if first:
            def keep(q, carry):
                p_high[q], p_low[q] = split(jnp.where(crossed, x_got[q], r_ref[q]))
                return carry
            lax.fori_loop(0, nq, keep, 0)
        reduce_chunk(nq - 1)

    def neighbours_in(first):
        def body(q, carry):
            @pl.when(has_up)
            def _():
                t_copy(0, q).wait_recv()

            @pl.when(has_down)
            def _():
                t_copy(1, q).wait_recv()

            @pl.when(has_down)
            def _():
                t_copy(0, q).wait_send()

            @pl.when(has_up)
            def _():
                t_copy(1, q).wait_send()
            return carry
        lax.fori_loop(0, nq, body, 0)
        for q in range(nq):
            both = t_got[0, q] + t_got[1, q]
            if first:
                sig[:, q * cq:(q + 1) * cq] += both
            else:
                for p in range(nq):
                    sig[q * rq:(q + 1) * rq, p * cq:(p + 1) * cq] += both[p * rq:(p + 1) * rq]
        return jnp.where(live(k), sig[...], 0.0)

    left_products(True)
    wait_many(klass, k_send, k_recv, no)
    right_products(True)
    sigma = neighbours_in(True)

    gathered[k] = sigma

    def member(dx, dz, dc):
        return ((x + dx) % nx) * 4 + ((zlo + dz) % 2) * 2 + (core + dc) % 2

    def g_copy(dx, dz, dc, to_x, to_z, to_c):
        block = gathered.at[member(nx - dx, dz, dc)]
        slot = ((dx + to_x) % nx) * 4 + ((dz + to_z) % 2) * 2 + (dc + to_c) % 2
        return pltpu.make_async_remote_copy(
            src_ref=block, dst_ref=block, send_sem=g_send.at[slot], recv_sem=g_recv.at[slot],
            device_id=(s, member(to_x, to_z, to_c)), device_id_type=MESH)

    def g_wait(dx, dz, dc):
        block = gathered.at[member(nx - dx, dz, dc)]
        slot = dx * 4 + dz * 2 + dc
        pltpu.make_async_remote_copy(
            src_ref=block, dst_ref=block, send_sem=g_send.at[slot], recv_sem=g_recv.at[slot],
            device_id=(s, member(0, 0, 1)), device_id_type=MESH).wait_recv()

    sends = []

    def g_start(*arguments):
        copy = g_copy(*arguments)
        copy.start()
        sends.append(copy)

    around = [1, nx - 1] + list(range(2, nx - 1))
    g_start(0, 0, 0, 0, 1, 0)
    for step in around:
        g_start(0, 0, 0, step, 0, 0)
    g_start(0, 0, 0, 0, 0, 1)
    op_start(0, jnp.sum(sigma * start_block(k)))
    g_wait(0, 1, 0)
    for step in around:
        g_start(0, 1, 0, step, 0, 0)
    g_start(0, 1, 0, 0, 0, 1)
    sec_start(1, op_finish(0))
    for dz in (0, 1):
        for dx in around:
            g_wait(dx, dz, 0)
            g_start(dx, dz, 0, 0, 0, 1)
    start_total = sec_finish(0)
    cross_total = sec_finish(1)
    scale = lax.rsqrt(start_total / cells + epsilon)
    rayleigh_one = cross_total * (scale * scale) / cells
    shift_by = jnp.max(rayleigh_one)
    for dz in (0, 1):
        for dx in range(nx):
            g_wait(dx, dz, 1)
    for copy in sends:
        copy.wait_send()

    def residual_block(block):
        return gathered[block] - shift_by * start_block(block)

    def fill_residual(block, total):
        value = residual_block(block)
        at = pl.ds(pl.multiple_of(block * share, share), share)
        v_high[at], v_low[at] = split(value)
        return total + jnp.sum((value * value).reshape(share // 8, 8, n), axis=0)

    squares = lax.fori_loop(0, no, fill_residual, jnp.zeros((8, n), F32))
    sec_start(2, jnp.full((8, 128), jnp.sum(squares), F32))

    left_products(False)
    right_products(False)
    residual_total = sec_finish(2)
    next_tile = scale * lax.rsqrt(residual_total * (scale * scale) / cells + epsilon)
    next_scale = jnp.max(next_tile)
    sigma = neighbours_in(False)
    residual = residual_block(k)
    op_start(1, jnp.sum(sigma * residual))
    nv_ref[0] = residual * next_scale
    out_sigma_ref[0] = sigma * next_scale
    sec_start(3, op_finish(1))
    rayleigh_two = sec_finish(3) * (next_tile * next_tile) / cells
    lane = lax.broadcasted_iota(jnp.int32, (8, 128), 1)
    proj_ref[...] = jnp.where(lane == 0, rayleigh_one, rayleigh_two)


def on_device(ns, state, left_ops, right_ops, charge, sizes):
    n = state.shape[1]
    no = lax.axis_size("op")
    share = n // no
    nq = CHUNKS
    rq, cq = share // nq, n // nq
    vmem = pltpu.VMEM
    dma = pltpu.SemaphoreType.DMA
    whole = pl.BlockSpec(memory_space=vmem)
    small = pl.BlockSpec(memory_space=pltpu.SMEM)
    nv, sigma, proj = pl.pallas_call(
        functools.partial(kernel, nq, ns),
        out_shape=[
            jax.ShapeDtypeStruct((1, share, n), F32),
            jax.ShapeDtypeStruct((1, share, n), F32),
            jax.ShapeDtypeStruct((8, 128), F32),
        ],
        in_specs=[whole, whole, whole, small, small],
        out_specs=[whole, whole, whole],
        scratch_shapes=[
            vmem((nq, cq, n), BF16), vmem((nq, cq, n), BF16),
            vmem((n, n), BF16), vmem((n, n), BF16),
            vmem((nq, cq, n), BF16), vmem((nq, cq, n), BF16),
            vmem((nq, cq, n), F32), vmem((nq, cq, n), F32), vmem((nq, cq, n), F32),
            vmem((nq, no, share, cq), F32), vmem((nq, no, share, cq), F32),
            vmem((2, nq, share, cq), F32), vmem((2, nq, share, cq), F32),
            vmem((share, n), F32), vmem((no, share, n), F32),
            vmem((no, 8, 128), F32), vmem((8, 128), F32),
            vmem((2, no, 8, 128), F32), vmem((4, ns, 8, 128), F32),
            dma((nq,)), dma((nq,)), dma((nq,)), dma((nq,)),
            dma((2, nq)), dma((2, nq)), dma((no,)), dma((no,)),
            dma, dma, dma((2,)), dma((2,)), dma((4,)), dma((4,)),
        ],
        compiler_params=pltpu.CompilerParams(
            collective_id=0, has_side_effects=True, vmem_limit_bytes=60 * 1024 * 1024),
        cost_estimate=pl.CostEstimate(flops=24 * n * n * n, bytes_accessed=12 * n * n, transcendentals=0),
    )(state.reshape(no, share, n), left_ops.reshape(no, share, n), right_ops.reshape(nq, cq, n), charge, sizes)
    return nv, sigma, proj[0, :2]


def solution(mesh):
    in_specs = (
        P("sec", None, None),
        P("op", "sec", None, None),
        P("op", "sec", None, None),
        P("op"),
        P("sec"),
    )
    out_specs = (P("sec", "op", None), P("sec", "op", None), P())
    return jax.shard_map(
        functools.partial(on_device, mesh.shape["sec"]), mesh=mesh, in_specs=in_specs, out_specs=out_specs,
        check_vma=False)
```

```python
import functools
import jax
import jax.numpy as jnp
from jax import lax
from jax.experimental import pallas as pl
from jax.experimental.pallas import tpu as pltpu
from jax.sharding import PartitionSpec as P

epsilon = 1e-06
CHUNKS = 4
F32 = jnp.float32
BF16 = jnp.bfloat16
MESH = pl.DeviceIdType.MESH


def split(x):
    high = x.astype(BF16)
    return high, (x - high.astype(F32)).astype(BF16)


def dot3(a_high, a_low, b_high, b_low, contract):
    def one(a, b):
        return lax.dot_general(a, b, (contract, ((), ())), preferred_element_type=F32)
    return one(a_high, b_high) + (one(a_high, b_low) + one(a_low, b_high))


def kernel(
    nq, ns, state_ref, l_ref, r_ref, charge_ref, sizes_ref,
    nv_ref, out_sigma_ref, proj_ref,
    l_high, l_low, v_high, v_low, p_high, p_low, x_own, x_sent, x_got,
    x_relay, y_out, y_got, z_out, z_got, t_out, t_got, sig, gathered, klass, op_got, sec_got,
    x_send, x_recv, w_send, w_recv, y_send, y_recv, z_send, z_recv, t_send, t_recv, g_send, g_recv,
    k_send, k_recv, op_send, op_recv, sec_send, sec_recv,
):
    no, share, n = state_ref.shape
    rq, cq = share // nq, n // nq
    s = lax.axis_index("sec")
    k = lax.axis_index("op")
    core = k % 2
    zlo = (k // 2) % 2
    x = k // 4
    nx = no // 4
    d = 1 - 2 * core
    dst, src = s + d, s - d
    has_dst = (dst >= 0) & (dst < ns)
    has_src = (src >= 0) & (src < ns)
    has_up = s < ns - 1
    has_down = s > 0
    charge = charge_ref[0]
    size = sizes_ref[0]
    cells = 1.0 * ns * n * n
    crossed = charge == -d

    barrier = pltpu.get_barrier_semaphore()

    def greet_op(j, carry):
        pl.semaphore_signal(barrier, inc=1, device_id=(s, (k + j) % no), device_id_type=MESH)
        return carry

    def greet_sec(j, carry):
        pl.semaphore_signal(barrier, inc=1, device_id=((s + j) % ns, k), device_id_type=MESH)
        return carry

    lax.fori_loop(1, no, greet_op, 0)
    lax.fori_loop(1, ns, greet_sec, 0)

    def member(dx, dz, dc):
        return ((x + dx) % nx) * 4 + ((zlo + dz) % 2) * 2 + (core + dc) % 2

    def greet_across(j, carry):
        to = ((s + j) % ns, member(0, 1, 0))
        pl.semaphore_signal(barrier, inc=1, device_id=to, device_id_type=MESH)
        return carry

    lax.fori_loop(1, ns, greet_across, 0)

    def op_copy(source, target, send, recv, j):
        return pltpu.make_async_remote_copy(
            src_ref=source, dst_ref=target.at[j], send_sem=send, recv_sem=recv,
            device_id=(s, (k + j) % no), device_id_type=MESH)

    def sec_copy(source, target, send, recv, j):
        return pltpu.make_async_remote_copy(
            src_ref=source, dst_ref=target.at[j], send_sem=send, recv_sem=recv,
            device_id=((s + j) % ns, k), device_id_type=MESH)

    def wait_many(target, send, recv, count):
        whole = target.at[pl.ds(1, count - 1)]
        copy = pltpu.make_async_remote_copy(
            src_ref=whole, dst_ref=whole, send_sem=send, recv_sem=recv,
            device_id=(s, (k + 1) % no), device_id_type=MESH)
        copy.wait_send()
        copy.wait_recv()

    def op_start(which, value):
        op_got[which, 0] = jnp.full((8, 128), value, F32)

        def body(j, carry):
            op_copy(op_got.at[which, 0], op_got.at[which], op_send.at[which], op_recv.at[which], j).start()
            return carry
        lax.fori_loop(1, no, body, 0)

    def op_finish(which):
        wait_many(op_got.at[which], op_send.at[which], op_recv.at[which], no)
        total = jnp.zeros((8, 128), F32)
        for i in range(no):
            total = total + op_got[which, (k + no - i) % no]
        return total

    def sec_start(which, tile):
        sec_got[which, 0] = tile

        def body(j, carry):
            sec_copy(sec_got.at[which, 0], sec_got.at[which], sec_send.at[which], sec_recv.at[which], j).start()
            return carry
        lax.fori_loop(1, ns, body, 0)

    def sec_finish(which):
        wait_many(sec_got.at[which], sec_send.at[which], sec_recv.at[which], ns)
        total = jnp.zeros((8, 128), F32)
        for i in range(ns):
            total = total + sec_got[which, (s + ns - i) % ns]
        return total

    def shifted(source, q):
        return pltpu.make_async_remote_copy(
            src_ref=source.at[q], dst_ref=x_got.at[q], send_sem=x_send.at[q], recv_sem=x_recv.at[q],
            device_id=((dst + ns) % ns, k), device_id_type=MESH)

    half = ns // 2
    at_edge = s == half - 1 + core
    relays = s == (ns - 1) * (1 - core)

    def to_relay(source, q):
        return pltpu.make_async_remote_copy(
            src_ref=source.at[q], dst_ref=x_relay.at[q // 2], send_sem=x_send.at[q], recv_sem=w_recv.at[q // 2],
            device_id=((ns - 1) * (1 - core), member(0, 1, 0)), device_id_type=MESH)

    def from_relay(q):
        return pltpu.make_async_remote_copy(
            src_ref=x_relay.at[q // 2], dst_ref=x_got.at[q], send_sem=w_send.at[q // 2], recv_sem=x_recv.at[q],
            device_id=(half - core, member(0, 1, 0)), device_id_type=MESH)

    def start_shift(source, q):
        by_relay = at_edge & (q % 2 == 1)

        @pl.when(by_relay)
        def _():
            to_relay(source, q).start()

        @pl.when(has_dst & jnp.logical_not(by_relay))
        def _():
            shifted(source, q).start()

    columns = lax.broadcasted_iota(jnp.int32, (share, n), 1) < size
    rows = lax.broadcasted_iota(jnp.int32, (share, n), 0)

    def live(block):
        return columns & (rows + block * share < size)

    def start_block(block):
        return jnp.where(live(block), state_ref[block], 0.0)

    def fill_start(block, total):
        value = start_block(block)
        at = pl.ds(pl.multiple_of(block * share, share), share)
        v_high[at], v_low[at] = split(value)
        return total + jnp.sum((value * value).reshape(share // 8, 8, n), axis=0)

    squares = lax.fori_loop(0, no, fill_start, jnp.zeros((8, n), F32))
    start_square = jnp.sum(squares)

    @pl.when(jnp.logical_not(has_src))
    def _():
        x_got[...] = jnp.zeros_like(x_got)

    @pl.when(jnp.logical_not(has_up))
    def _():
        t_got[0] = jnp.zeros(t_got.shape[1:], F32)

    @pl.when(jnp.logical_not(has_down))
    def _():
        t_got[1] = jnp.zeros(t_got.shape[1:], F32)

    pl.semaphore_wait(barrier, no - 1 + 2 * (ns - 1))

    klass[0] = jnp.full((8, 128), jnp.where(crossed, 1.0, 0.0), F32)

    def x_copy(source, target, send, recv, j):
        return pltpu.make_async_remote_copy(
            src_ref=source, dst_ref=target.at[j], send_sem=send, recv_sem=recv,
            device_id=(s, member(j, 0, 0)), device_id_type=MESH)

    for j in range(1, nx):
        x_copy(klass.at[0], klass, k_send, k_recv, j).start()
    sec_start(0, jnp.full((8, 128), start_square, F32))

    def left_products(first):
        def body(q, carry):
            if first:
                at = pl.ds(pl.multiple_of(q * rq, rq), rq)
                high, low = split(l_ref[:, at, :].reshape(no * rq, n))
                l_high[q] = high
                l_low[q] = low
            else:
                high, low = l_high[q], l_low[q]
            product = dot3(high, low, v_high[...], v_low[...], ((1,), (0,)))
            x_own[q] = product
            if first:
                right = r_ref[q]
                x_sent[q] = jnp.where(charge == d, product, right)
                p_high[q], p_low[q] = split(jnp.where(crossed, product, right))

            start_shift(x_sent if first else x_own, q)
            return carry
        lax.fori_loop(0, nq, body, 0)

    def t_copy(way, q):
        to = s - 1 if way == 0 else s + 1
        return pltpu.make_async_remote_copy(
            src_ref=t_out.at[way, q], dst_ref=t_got.at[way, q], send_sem=t_send.at[way, q],
            recv_sem=t_recv.at[way, q], device_id=((to + ns) % ns, k), device_id_type=MESH)

    def reduce_x(q):
        wait_many(y_got.at[q], y_send.at[q], y_recv.at[q], nx)
        flags = [jnp.concatenate([klass[j]] * (cq // 128), axis=1)[None] for j in range(nx)]
        for m in range(4):
            parts = [y_out[q, x * 4 + m]] + [y_got[q, j, m] for j in range(1, nx)]
            parts = [part.reshape(share // 8, 8, cq) for part in parts]
            there = [part * flag for part, flag in zip(parts, flags)]
            here = [part - one for part, one in zip(parts, there)]
            z_out[q, m, 0] = sum(here[1:], here[0]).reshape(share, cq)
            z_out[q, m, 1] = sum(there[1:], there[0]).reshape(share, cq)
        for j in range(1, 4):
            z_copy(q, j).start()

    def z_copy(q, j):
        to = (k % 4 + j) % 4
        return pltpu.make_async_remote_copy(
            src_ref=z_out.at[q, to], dst_ref=z_got.at[q, j], send_sem=z_send.at[q], recv_sem=z_recv.at[q],
            device_id=(s, x * 4 + to), device_id_type=MESH)

    def reduce_z(q):
        wait_many(z_got.at[q], z_send.at[q], z_recv.at[q], 4)
        own = z_out[q, k % 4]
        got = [z_got[q, j] for j in range(1, 4)]
        here = (own[0] + got[1][0]) + (got[0][0] + got[2][0])
        same = own[1] + got[1][1]
        other = got[0][1] + got[2][1]
        at = pl.ds(pl.multiple_of(q * rq, rq), rq)
        for p in range(nq):
            sig[at, p * cq:(p + 1) * cq] = here[p * rq:(p + 1) * rq]
        t_out[0, q] = jnp.where(core == 0, same, other)
        t_out[1, q] = jnp.where(core == 0, other, same)

        @pl.when(has_down)
        def _():
            t_copy(0, q).start()

        @pl.when(has_up)
        def _():
            t_copy(1, q).start()

    def right_products(first):
        def body(q, carry):
            @pl.when(relays & (q % 2 == 1))
            def _():
                to_relay(x_sent, q).wait_recv()
                from_relay(q).start()

            @pl.when(has_src)
            def _():
                shifted(x_sent, q).wait_recv()
            use_own = charge == 0 if first else charge != d
            high, low = split(jnp.where(use_own, x_own[q], x_got[q]))
            for p in range(nq):
                block = dot3(high, low, p_high[p], p_low[p], ((1,), (1,)))
                if first:
                    block = jnp.where(crossed, block.T, block)
                y_out[q, :, p * rq:(p + 1) * rq, :] = block.reshape(no, rq, cq)

            for j in range(1, nx):
                block = y_out.at[q, pl.ds(((x + j) % nx) * 4, 4)]
                x_copy(block, y_got.at[q], y_send.at[q], y_recv.at[q], j).start()

            @pl.when(q > 0)
            def _():
                reduce_x(q - 1)

            @pl.when(q > 1)
            def _():
                reduce_z(q - 2)
            return carry
        lax.fori_loop(0, nq, body, 0)

        @pl.when(has_dst)
        def _():
            def done(q, carry):
                shifted(x_sent if first else x_own, q).wait_send()
                return carry
            lax.fori_loop(0, nq, done, 0)

        @pl.when(relays)
        def _():
            def passed(i, carry):
                from_relay(2 * i + 1).wait_send()
                return carry
            lax.fori_loop(0, nq // 2, passed, 0)
        if first:
            def keep(q, carry):
                p_high[q], p_low[q] = split(jnp.where(crossed, x_got[q], r_ref[q]))
                return carry
            lax.fori_loop(0, nq, keep, 0)
        reduce_x(nq - 1)
        reduce_z(nq - 2)
        reduce_z(nq - 1)

    def neighbours_in(first):
        def body(q, carry):
            @pl.when(has_up)
            def _():
                t_copy(0, q).wait_recv()

            @pl.when(has_down)
            def _():
                t_copy(1, q).wait_recv()

            @pl.when(has_down)
            def _():
                t_copy(0, q).wait_send()

            @pl.when(has_up)
            def _():
                t_copy(1, q).wait_send()
            return carry
        lax.fori_loop(0, nq, body, 0)
        for q in range(nq):
            both = t_got[0, q] + t_got[1, q]
            if first:
                sig[:, q * cq:(q + 1) * cq] += both
            else:
                for p in range(nq):
                    sig[q * rq:(q + 1) * rq, p * cq:(p + 1) * cq] += both[p * rq:(p + 1) * rq]
        return jnp.where(live(k), sig[...], 0.0)

    left_products(True)
    wait_many(klass, k_send, k_recv, nx)
    right_products(True)
    sigma = neighbours_in(True)

    gathered[k] = sigma

    def g_copy(dx, dz, dc, to_x, to_z, to_c):
        block = gathered.at[member(nx - dx, dz, dc)]
        slot = ((dx + to_x) % nx) * 4 + ((dz + to_z) % 2) * 2 + (dc + to_c) % 2
        return pltpu.make_async_remote_copy(
            src_ref=block, dst_ref=block, send_sem=g_send.at[slot], recv_sem=g_recv.at[slot],
            device_id=(s, member(to_x, to_z, to_c)), device_id_type=MESH)

    def g_wait(dx, dz, dc):
        block = gathered.at[member(nx - dx, dz, dc)]
        slot = dx * 4 + dz * 2 + dc
        pltpu.make_async_remote_copy(
            src_ref=block, dst_ref=block, send_sem=g_send.at[slot], recv_sem=g_recv.at[slot],
            device_id=(s, member(0, 0, 1)), device_id_type=MESH).wait_recv()

    sends = []

    def g_start(*arguments):
        copy = g_copy(*arguments)
        copy.start()
        sends.append(copy)

    around = [1, nx - 1] + list(range(2, nx - 1))
    g_start(0, 0, 0, 0, 1, 0)
    for step in around:
        g_start(0, 0, 0, step, 0, 0)
    g_start(0, 0, 0, 0, 0, 1)
    op_start(0, jnp.sum(sigma * start_block(k)))
    g_wait(0, 1, 0)
    for step in around:
        g_start(0, 1, 0, step, 0, 0)
    g_start(0, 1, 0, 0, 0, 1)
    sec_start(1, op_finish(0))
    for dz in (0, 1):
        for dx in around:
            g_wait(dx, dz, 0)
            g_start(dx, dz, 0, 0, 0, 1)
    start_total = sec_finish(0)
    cross_total = sec_finish(1)
    scale = lax.rsqrt(start_total / cells + epsilon)
    rayleigh_one = cross_total * (scale * scale) / cells
    shift_by = jnp.max(rayleigh_one)
    for dz in (0, 1):
        for dx in range(nx):
            g_wait(dx, dz, 1)
    for copy in sends:
        copy.wait_send()

    def residual_block(block):
        return gathered[block] - shift_by * start_block(block)

    def fill_residual(block, total):
        value = residual_block(block)
        at = pl.ds(pl.multiple_of(block * share, share), share)
        v_high[at], v_low[at] = split(value)
        return total + jnp.sum((value * value).reshape(share // 8, 8, n), axis=0)

    squares = lax.fori_loop(0, no, fill_residual, jnp.zeros((8, n), F32))
    sec_start(2, jnp.full((8, 128), jnp.sum(squares), F32))

    left_products(False)
    right_products(False)
    residual_total = sec_finish(2)
    next_tile = scale * lax.rsqrt(residual_total * (scale * scale) / cells + epsilon)
    next_scale = jnp.max(next_tile)
    sigma = neighbours_in(False)
    residual = residual_block(k)
    op_start(1, jnp.sum(sigma * residual))
    nv_ref[0] = residual * next_scale
    out_sigma_ref[0] = sigma * next_scale
    sec_start(3, op_finish(1))
    rayleigh_two = sec_finish(3) * (next_tile * next_tile) / cells
    lane = lax.broadcasted_iota(jnp.int32, (8, 128), 1)
    proj_ref[...] = jnp.where(lane == 0, rayleigh_one, rayleigh_two)


def on_device(ns, state, left_ops, right_ops, charge, sizes):
    n = state.shape[1]
    no = lax.axis_size("op")
    share = n // no
    nq = CHUNKS
    rq, cq = share // nq, n // nq
    vmem = pltpu.VMEM
    dma = pltpu.SemaphoreType.DMA
    whole = pl.BlockSpec(memory_space=vmem)
    small = pl.BlockSpec(memory_space=pltpu.SMEM)
    nv, sigma, proj = pl.pallas_call(
        functools.partial(kernel, nq, ns),
        out_shape=[
            jax.ShapeDtypeStruct((1, share, n), F32),
            jax.ShapeDtypeStruct((1, share, n), F32),
            jax.ShapeDtypeStruct((8, 128), F32),
        ],
        in_specs=[whole, whole, whole, small, small],
        out_specs=[whole, whole, whole],
        scratch_shapes=[
            vmem((nq, cq, n), BF16), vmem((nq, cq, n), BF16),
            vmem((n, n), BF16), vmem((n, n), BF16),
            vmem((nq, cq, n), BF16), vmem((nq, cq, n), BF16),
            vmem((nq, cq, n), F32), vmem((nq, cq, n), F32), vmem((nq, cq, n), F32),
            vmem((nq // 2, cq, n), F32),
            vmem((nq, no, share, cq), F32), vmem((nq, no // 4, 4, share, cq), F32),
            vmem((nq, 4, 2, share, cq), F32), vmem((nq, 4, 2, share, cq), F32),
            vmem((2, nq, share, cq), F32), vmem((2, nq, share, cq), F32),
            vmem((share, n), F32), vmem((no, share, n), F32),
            vmem((no // 4, 8, 128), F32),
            vmem((2, no, 8, 128), F32), vmem((4, ns, 8, 128), F32),
            dma((nq,)), dma((nq,)), dma((nq // 2,)), dma((nq // 2,)),
            dma((nq,)), dma((nq,)), dma((nq,)), dma((nq,)),
            dma((2, nq)), dma((2, nq)), dma((no,)), dma((no,)),
            dma, dma, dma((2,)), dma((2,)), dma((4,)), dma((4,)),
        ],
        compiler_params=pltpu.CompilerParams(
            collective_id=0, has_side_effects=True, vmem_limit_bytes=60 * 1024 * 1024),
        cost_estimate=pl.CostEstimate(flops=24 * n * n * n, bytes_accessed=12 * n * n, transcendentals=0),
    )(state.reshape(no, share, n), left_ops.reshape(no, share, n), right_ops.reshape(nq, cq, n), charge, sizes)
    return nv, sigma, proj[0, :2]


def solution(mesh):
    in_specs = (
        P("sec", None, None),
        P("op", "sec", None, None),
        P("op", "sec", None, None),
        P("op"),
        P("sec"),
    )
    out_specs = (P("sec", "op", None), P("sec", "op", None), P())
    return jax.shard_map(
        functools.partial(on_device, mesh.shape["sec"]), mesh=mesh, in_specs=in_specs, out_specs=out_specs,
        check_vma=False)
```

```python
import functools
import jax
import jax.numpy as jnp
from jax import lax
from jax.experimental import pallas as pl
from jax.experimental.pallas import tpu as pltpu
from jax.sharding import PartitionSpec as P

epsilon = 1e-06
CHUNKS = 8
X_LAG = 2
Z_LAG = 4
F32 = jnp.float32
BF16 = jnp.bfloat16
MESH = pl.DeviceIdType.MESH


def split(x):
    high = x.astype(BF16)
    return high, (x - high.astype(F32)).astype(BF16)


def dot3(a_high, a_low, b_high, b_low, contract):
    def one(a, b):
        return lax.dot_general(a, b, (contract, ((), ())), preferred_element_type=F32)
    return one(a_high, b_high) + (one(a_high, b_low) + one(a_low, b_high))


def kernel(
    nq, ns, state_in, l_in, r_in, charge_ref, sizes_ref,
    nv_ref, out_sigma_ref, proj_ref,
    state_ref, l_ref, r_ref, l_high, l_low, v_high, v_low, p_high, p_low, x_own, x_sent, x_got,
    x_relay, y_out, y_got, z_out, z_got, t_out, t_got, sig, gathered, klass, op_got, sec_got,
    x_send, x_recv, w_send, w_recv, y_send, y_recv, z_send, z_recv, t_send, t_recv, g_send, g_recv,
    k_send, k_recv, op_send, op_recv, sec_send, sec_recv,
    in_sem,
):
    no, share, n = state_ref.shape
    rq, cq = share // nq, n // nq

    def l_load(q):
        at = pl.ds(pl.multiple_of(q * rq, rq), rq)
        return pltpu.make_async_copy(l_in.at[:, at], l_ref.at[:, at], in_sem.at[1 + 2 * q])

    def r_load(q):
        return pltpu.make_async_copy(r_in.at[q], r_ref.at[q], in_sem.at[2 + 2 * q])

    state_load = pltpu.make_async_copy(state_in, state_ref, in_sem.at[0])
    state_load.start()

    def load(q, carry):
        l_load(q).start()
        r_load(q).start()
        return carry
    lax.fori_loop(0, nq, load, 0)
    s = lax.axis_index("sec")
    k = lax.axis_index("op")
    core = k % 2
    zlo = (k // 2) % 2
    x = k // 4
    nx = no // 4
    d = 1 - 2 * core
    dst, src = s + d, s - d
    has_dst = (dst >= 0) & (dst < ns)
    has_src = (src >= 0) & (src < ns)
    has_up = s < ns - 1
    has_down = s > 0
    charge = charge_ref[0]
    size = sizes_ref[0]
    cells = 1.0 * ns * n * n
    crossed = charge == -d

    barrier = pltpu.get_barrier_semaphore()

    def greet_op(j, carry):
        pl.semaphore_signal(barrier, inc=1, device_id=(s, (k + j) % no), device_id_type=MESH)
        return carry

    def greet_sec(j, carry):
        pl.semaphore_signal(barrier, inc=1, device_id=((s + j) % ns, k), device_id_type=MESH)
        return carry

    lax.fori_loop(1, no, greet_op, 0)
    lax.fori_loop(1, ns, greet_sec, 0)

    def member(dx, dz, dc):
        return ((x + dx) % nx) * 4 + ((zlo + dz) % 2) * 2 + (core + dc) % 2

    def greet_across(j, carry):
        to = ((s + j) % ns, member(0, 1, 0))
        pl.semaphore_signal(barrier, inc=1, device_id=to, device_id_type=MESH)
        return carry

    lax.fori_loop(1, ns, greet_across, 0)

    def op_copy(source, target, send, recv, j):
        return pltpu.make_async_remote_copy(
            src_ref=source, dst_ref=target.at[j], send_sem=send, recv_sem=recv,
            device_id=(s, (k + j) % no), device_id_type=MESH)

    def sec_copy(source, target, send, recv, j):
        return pltpu.make_async_remote_copy(
            src_ref=source, dst_ref=target.at[j], send_sem=send, recv_sem=recv,
            device_id=((s + j) % ns, k), device_id_type=MESH)

    def wait_many(target, send, recv, count):
        whole = target.at[pl.ds(1, count - 1)]
        copy = pltpu.make_async_remote_copy(
            src_ref=whole, dst_ref=whole, send_sem=send, recv_sem=recv,
            device_id=(s, (k + 1) % no), device_id_type=MESH)
        copy.wait_send()
        copy.wait_recv()

    def op_start(which, value):
        op_got[which, 0] = jnp.full((8, 128), value, F32)

        def body(j, carry):
            op_copy(op_got.at[which, 0], op_got.at[which], op_send.at[which], op_recv.at[which], j).start()
            return carry
        lax.fori_loop(1, no, body, 0)

    def op_finish(which):
        wait_many(op_got.at[which], op_send.at[which], op_recv.at[which], no)
        total = jnp.zeros((8, 128), F32)
        for i in range(no):
            total = total + op_got[which, (k + no - i) % no]
        return total

    def sec_start(which, tile):
        sec_got[which, 0] = tile

        def body(j, carry):
            sec_copy(sec_got.at[which, 0], sec_got.at[which], sec_send.at[which], sec_recv.at[which], j).start()
            return carry
        lax.fori_loop(1, ns, body, 0)

    def sec_finish(which):
        wait_many(sec_got.at[which], sec_send.at[which], sec_recv.at[which], ns)
        total = jnp.zeros((8, 128), F32)
        for i in range(ns):
            total = total + sec_got[which, (s + ns - i) % ns]
        return total

    def shifted(source, q):
        return pltpu.make_async_remote_copy(
            src_ref=source.at[q], dst_ref=x_got.at[q], send_sem=x_send.at[q], recv_sem=x_recv.at[q],
            device_id=((dst + ns) % ns, k), device_id_type=MESH)

    half = ns // 2
    at_edge = s == half - 1 + core
    relays = s == (ns - 1) * (1 - core)

    def to_relay(source, q):
        return pltpu.make_async_remote_copy(
            src_ref=source.at[q], dst_ref=x_relay.at[q // 2], send_sem=x_send.at[q], recv_sem=w_recv.at[q // 2],
            device_id=((ns - 1) * (1 - core), member(0, 1, 0)), device_id_type=MESH)

    def from_relay(q):
        return pltpu.make_async_remote_copy(
            src_ref=x_relay.at[q // 2], dst_ref=x_got.at[q], send_sem=w_send.at[q // 2], recv_sem=x_recv.at[q],
            device_id=(half - core, member(0, 1, 0)), device_id_type=MESH)

    def start_shift(source, q):
        by_relay = at_edge & (q % 2 == 1)

        @pl.when(by_relay)
        def _():
            to_relay(source, q).start()

        @pl.when(has_dst & jnp.logical_not(by_relay))
        def _():
            shifted(source, q).start()

    columns = lax.broadcasted_iota(jnp.int32, (share, n), 1) < size
    rows = lax.broadcasted_iota(jnp.int32, (share, n), 0)

    def live(block):
        return columns & (rows + block * share < size)

    def start_block(block):
        return jnp.where(live(block), state_ref[block], 0.0)

    def fill_start(block, total):
        value = start_block(block)
        at = pl.ds(pl.multiple_of(block * share, share), share)
        v_high[at], v_low[at] = split(value)
        return total + jnp.sum((value * value).reshape(share // 8, 8, n), axis=0)

    state_load.wait()
    squares = lax.fori_loop(0, no, fill_start, jnp.zeros((8, n), F32))
    start_square = jnp.sum(squares)

    @pl.when(jnp.logical_not(has_src))
    def _():
        x_got[...] = jnp.zeros_like(x_got)

    @pl.when(jnp.logical_not(has_up))
    def _():
        t_got[0] = jnp.zeros(t_got.shape[1:], F32)

    @pl.when(jnp.logical_not(has_down))
    def _():
        t_got[1] = jnp.zeros(t_got.shape[1:], F32)

    pl.semaphore_wait(barrier, no - 1 + 2 * (ns - 1))

    klass[0] = jnp.full((8, 128), jnp.where(crossed, 1.0, 0.0), F32)

    def x_copy(source, target, send, recv, j):
        return pltpu.make_async_remote_copy(
            src_ref=source, dst_ref=target.at[j], send_sem=send, recv_sem=recv,
            device_id=(s, member(j, 0, 0)), device_id_type=MESH)

    for j in range(1, nx):
        x_copy(klass.at[0], klass, k_send, k_recv, j).start()

    pair = max(1, 256 // cq)

    def left_products(first):
        def body(block, carry):
            base = block * pair
            if first:
                for i in range(pair):
                    l_load(base + i).wait()
                    r_load(base + i).wait()
                    at = pl.ds(pl.multiple_of((base + i) * rq, rq), rq)
                    l_high[base + i], l_low[base + i] = split(l_ref[:, at, :].reshape(no * rq, n))
            both = pl.ds(base, pair)
            high, low = l_high[both].reshape(pair * cq, n), l_low[both].reshape(pair * cq, n)
            wide = dot3(high, low, v_high[...], v_low[...], ((1,), (0,)))
            for i in range(pair):
                q = base + i
                product = wide[i * cq:(i + 1) * cq]
                x_own[q] = product
                if first:
                    right = r_ref[q]
                    x_sent[q] = jnp.where(charge == d, product, right)
                    p_high[q], p_low[q] = split(jnp.where(crossed, product, right))
                start_shift(x_sent if first else x_own, q)
            return carry
        lax.fori_loop(0, nq // pair, body, 0)

    def t_copy(way, q):
        to = s - 1 if way == 0 else s + 1
        return pltpu.make_async_remote_copy(
            src_ref=t_out.at[way, q], dst_ref=t_got.at[way, q], send_sem=t_send.at[way, q],
            recv_sem=t_recv.at[way, q], device_id=((to + ns) % ns, k), device_id_type=MESH)

    def reduce_x(q):
        wait_many(y_got.at[q], y_send.at[q], y_recv.at[q], nx)
        flags = [jnp.concatenate([klass[j]] * (cq // 128), axis=1)[None] for j in range(nx)]
        for m in range(4):
            parts = [y_out[q, x * 4 + m]] + [y_got[q, j, m] for j in range(1, nx)]
            parts = [part.reshape(share // 8, 8, cq) for part in parts]
            there = [part * flag for part, flag in zip(parts, flags)]
            here = [part - one for part, one in zip(parts, there)]
            z_out[q, m, 0] = sum(here[1:], here[0]).reshape(share, cq)
            z_out[q, m, 1] = sum(there[1:], there[0]).reshape(share, cq)
        for j in range(1, 4):
            z_copy(q, j).start()

    def z_copy(q, j):
        to = (k % 4 + j) % 4
        return pltpu.make_async_remote_copy(
            src_ref=z_out.at[q, to], dst_ref=z_got.at[q, j], send_sem=z_send.at[q], recv_sem=z_recv.at[q],
            device_id=(s, x * 4 + to), device_id_type=MESH)

    def reduce_z(q):
        wait_many(z_got.at[q], z_send.at[q], z_recv.at[q], 4)
        own = z_out[q, k % 4]
        got = [z_got[q, j] for j in range(1, 4)]
        here = (own[0] + got[1][0]) + (got[0][0] + got[2][0])
        same = own[1] + got[1][1]
        other = got[0][1] + got[2][1]
        at = pl.ds(pl.multiple_of(q * rq, rq), rq)
        for p in range(nq):
            sig[at, p * cq:(p + 1) * cq] = here[p * rq:(p + 1) * rq]
        t_out[0, q] = jnp.where(core == 0, same, other)
        t_out[1, q] = jnp.where(core == 0, other, same)

        @pl.when(has_down)
        def _():
            t_copy(0, q).start()

        @pl.when(has_up)
        def _():
            t_copy(1, q).start()

    def right_products(first):
        def body(q, carry):
            @pl.when(relays & (q < nq // 2))
            def _():
                to_relay(x_sent, 2 * q + 1).wait_recv()
                from_relay(2 * q + 1).start()

            @pl.when(has_src)
            def _():
                shifted(x_sent, q).wait_recv()
            use_own = charge == 0 if first else charge != d
            high, low = split(jnp.where(use_own, x_own[q], x_got[q]))
            group = max(1, 256 // cq)
            for start in range(0, nq, group):
                at = pl.ds(start, group)
                wide = dot3(
                    high, low, p_high[at].reshape(group * cq, n), p_low[at].reshape(group * cq, n), ((1,), (1,)))
                for i in range(group):
                    p = start + i
                    block = wide[:, i * cq:(i + 1) * cq]
                    if first:
                        block = jnp.where(crossed, block.T, block)
                    y_out[q, :, p * rq:(p + 1) * rq, :] = block.reshape(no, rq, cq)

            for j in range(1, nx):
                block = y_out.at[q, pl.ds(((x + j) % nx) * 4, 4)]
                x_copy(block, y_got.at[q], y_send.at[q], y_recv.at[q], j).start()

            drain(q, 0)
            return carry

        def drain(q, carry):
            @pl.when((q >= X_LAG) & (q < nq + X_LAG))
            def _():
                reduce_x(q - X_LAG)

            @pl.when(q >= Z_LAG)
            def _():
                reduce_z(q - Z_LAG)
            return carry
        lax.fori_loop(0, nq, body, 0)

        @pl.when(has_dst)
        def _():
            def done(q, carry):
                shifted(x_sent if first else x_own, q).wait_send()
                return carry
            lax.fori_loop(0, nq, done, 0)

        @pl.when(relays)
        def _():
            def passed(i, carry):
                from_relay(2 * i + 1).wait_send()
                return carry
            lax.fori_loop(0, nq // 2, passed, 0)
        if first:
            def keep(q, carry):
                p_high[q], p_low[q] = split(jnp.where(crossed, x_got[q], r_ref[q]))
                return carry
            lax.fori_loop(0, nq, keep, 0)
        lax.fori_loop(nq, nq + Z_LAG, drain, 0)

    def neighbours_in(first):
        def body(q, carry):
            @pl.when(has_up)
            def _():
                t_copy(0, q).wait_recv()

            @pl.when(has_down)
            def _():
                t_copy(1, q).wait_recv()

            @pl.when(has_down)
            def _():
                t_copy(0, q).wait_send()

            @pl.when(has_up)
            def _():
                t_copy(1, q).wait_send()
            return carry
        lax.fori_loop(0, nq, body, 0)
        for q in range(nq):
            both = t_got[0, q] + t_got[1, q]
            if first:
                sig[:, q * cq:(q + 1) * cq] += both
            else:
                for p in range(nq):
                    sig[q * rq:(q + 1) * rq, p * cq:(p + 1) * cq] += both[p * rq:(p + 1) * rq]
        return jnp.where(live(k), sig[...], 0.0)

    left_products(True)
    sec_start(0, jnp.full((8, 128), start_square, F32))
    wait_many(klass, k_send, k_recv, nx)
    right_products(True)
    sigma = neighbours_in(True)

    gathered[k] = sigma

    def g_block(dx, dz, dc, part):
        block = member(nx - dx, dz, dc)
        if part is None:
            return gathered.at[block]
        return gathered.at[block, pl.ds(part * (share // 2), share // 2)]

    def g_copy(dx, dz, dc, to_x, to_z, to_c, part=None):
        block = g_block(dx, dz, dc, part)
        slot = ((dx + to_x) % nx) * 4 + ((dz + to_z) % 2) * 2 + (dc + to_c) % 2
        slot = no + dx if part == 1 else slot
        return pltpu.make_async_remote_copy(
            src_ref=block, dst_ref=block, send_sem=g_send.at[slot], recv_sem=g_recv.at[slot],
            device_id=(s, member(to_x, to_z, to_c)), device_id_type=MESH)

    def g_wait(dx, dz, dc, part=None):
        block = g_block(dx, dz, dc, part)
        slot = no + dx if part == 1 else dx * 4 + dz * 2 + dc
        pltpu.make_async_remote_copy(
            src_ref=block, dst_ref=block, send_sem=g_send.at[slot], recv_sem=g_recv.at[slot],
            device_id=(s, member(0, 0, 1)), device_id_type=MESH).wait_recv()

    sends = []

    def g_start(*arguments):
        copy = g_copy(*arguments)
        copy.start()
        sends.append(copy)

    around = [1, nx - 1] + list(range(2, nx - 1))
    g_start(0, 0, 0, 0, 1, 0)
    for step in around:
        g_start(0, 0, 0, step, 0, 0)
    g_start(0, 0, 0, 0, 0, 1)
    op_start(0, jnp.sum(sigma * start_block(k)))
    g_wait(0, 1, 0)
    for step in around:
        g_start(0, 1, 0, step, 0, 0, 0)
    g_start(0, 1, 0, 0, 0, 1)
    sec_start(1, op_finish(0))
    for dx in around:
        g_wait(dx, 0, 0)
        g_start(dx, 0, 0, 0, 1, 0, 1)
        g_start(dx, 0, 0, 0, 0, 1)
    for dx in around:
        g_wait(dx, 1, 0, 0)
        g_wait(dx, 1, 0, 1)
        g_start(dx, 1, 0, 0, 0, 1)
    start_total = sec_finish(0)
    cross_total = sec_finish(1)
    scale = lax.rsqrt(start_total / cells + epsilon)
    rayleigh_one = cross_total * (scale * scale) / cells
    shift_by = jnp.max(rayleigh_one)
    for dz in (0, 1):
        for dx in range(nx):
            g_wait(dx, dz, 1)
    for copy in sends:
        copy.wait_send()

    def residual_block(block):
        return gathered[block] - shift_by * start_block(block)

    def fill_residual(block, total):
        value = residual_block(block)
        at = pl.ds(pl.multiple_of(block * share, share), share)
        v_high[at], v_low[at] = split(value)
        return total + jnp.sum((value * value).reshape(share // 8, 8, n), axis=0)

    squares = lax.fori_loop(0, no, fill_residual, jnp.zeros((8, n), F32))

    left_products(False)
    sec_start(2, jnp.full((8, 128), jnp.sum(squares), F32))
    right_products(False)
    residual_total = sec_finish(2)
    next_tile = scale * lax.rsqrt(residual_total * (scale * scale) / cells + epsilon)
    next_scale = jnp.max(next_tile)
    sigma = neighbours_in(False)
    residual = residual_block(k)
    op_start(1, jnp.sum(sigma * residual))
    nv_ref[0] = residual * next_scale
    out_sigma_ref[0] = sigma * next_scale
    sec_start(3, op_finish(1))
    rayleigh_two = sec_finish(3) * (next_tile * next_tile) / cells
    lane = lax.broadcasted_iota(jnp.int32, (8, 128), 1)
    proj_ref[...] = jnp.where(lane == 0, rayleigh_one, rayleigh_two)


def on_device(ns, state, left_ops, right_ops, charge, sizes):
    n = state.shape[1]
    no = lax.axis_size("op")
    share = n // no
    nq = CHUNKS
    rq, cq = share // nq, n // nq
    vmem = pltpu.VMEM
    dma = pltpu.SemaphoreType.DMA
    whole = pl.BlockSpec(memory_space=vmem)
    far = pl.BlockSpec(memory_space=pl.ANY)
    small = pl.BlockSpec(memory_space=pltpu.SMEM)
    nv, sigma, proj = pl.pallas_call(
        functools.partial(kernel, nq, ns),
        out_shape=[
            jax.ShapeDtypeStruct((1, share, n), F32),
            jax.ShapeDtypeStruct((1, share, n), F32),
            jax.ShapeDtypeStruct((8, 128), F32),
        ],
        in_specs=[far, far, far, small, small],
        out_specs=[whole, whole, whole],
        scratch_shapes=[
            vmem((no, share, n), F32), vmem((no, share, n), F32), vmem((nq, cq, n), F32),
            vmem((nq, cq, n), BF16), vmem((nq, cq, n), BF16),
            vmem((n, n), BF16), vmem((n, n), BF16),
            vmem((nq, cq, n), BF16), vmem((nq, cq, n), BF16),
            vmem((nq, cq, n), F32), vmem((nq, cq, n), F32), vmem((nq, cq, n), F32),
            vmem((nq // 2, cq, n), F32),
            vmem((nq, no, share, cq), F32), vmem((nq, no // 4, 4, share, cq), F32),
            vmem((nq, 4, 2, share, cq), F32), vmem((nq, 4, 2, share, cq), F32),
            vmem((2, nq, share, cq), F32), vmem((2, nq, share, cq), F32),
            vmem((share, n), F32), vmem((no, share, n), F32),
            vmem((no // 4, 8, 128), F32),
            vmem((2, no, 8, 128), F32), vmem((4, ns, 8, 128), F32),
            dma((nq,)), dma((nq,)), dma((nq // 2,)), dma((nq // 2,)),
            dma((nq,)), dma((nq,)), dma((nq,)), dma((nq,)),
            dma((2, nq)), dma((2, nq)), dma((no + no // 4,)), dma((no + no // 4,)),
            dma, dma, dma((2,)), dma((2,)), dma((4,)), dma((4,)),
            dma((1 + 2 * nq,)),
        ],
        compiler_params=pltpu.CompilerParams(
            collective_id=0, has_side_effects=True, vmem_limit_bytes=60 * 1024 * 1024),
        cost_estimate=pl.CostEstimate(flops=24 * n * n * n, bytes_accessed=12 * n * n, transcendentals=0),
    )(state.reshape(no, share, n), left_ops.reshape(no, share, n), right_ops.reshape(nq, cq, n), charge, sizes)
    return nv, sigma, proj[0, :2]


def solution(mesh):
    in_specs = (
        P("sec", None, None),
        P("op", "sec", None, None),
        P("op", "sec", None, None),
        P("op"),
        P("sec"),
    )
    out_specs = (P("sec", "op", None), P("sec", "op", None), P())
    return jax.shard_map(
        functools.partial(on_device, mesh.shape["sec"]), mesh=mesh, in_specs=in_specs, out_specs=out_specs,
        check_vma=False)
```

```python
import functools
import jax
import jax.numpy as jnp
from jax import lax
from jax.experimental import pallas as pl
from jax.experimental.pallas import tpu as pltpu
from jax.sharding import PartitionSpec as P

epsilon = 1e-06
CHUNKS = 8
X_LAG = 2
Z_LAG = 4
F32 = jnp.float32
BF16 = jnp.bfloat16
MESH = pl.DeviceIdType.MESH


def split(x):
    high = x.astype(BF16)
    return high, (x - high.astype(F32)).astype(BF16)


def dot3(a_high, a_low, b_high, b_low, contract):
    def one(a, b):
        return lax.dot_general(a, b, (contract, ((), ())), preferred_element_type=F32)
    return one(a_high, b_high) + (one(a_high, b_low) + one(a_low, b_high))


def kernel(
    nq, ns, state_in, l_in, r_in, charge_ref, sizes_ref,
    nv_ref, out_sigma_ref, proj_ref,
    state_ref, l_ref, r_ref, l_high, l_low, v_high, v_low, p_high, p_low, x_own, x_sent, x_got,
    x_relay, y_out, y_got, z_out, z_got, t_out, t_got, sig, gathered, klass, squares, op_got, sec_got,
    x_send, x_recv, w_send, w_recv, y_send, y_recv, z_send, z_recv, t_send, t_recv, g_send, g_recv,
    k_send, k_recv, op_send, op_recv, sec_send, sec_recv,
    in_sem,
):
    no, share, n = state_ref.shape
    rq, cq = share // nq, n // nq

    def l_load(q):
        at = pl.ds(pl.multiple_of(q * rq, rq), rq)
        return pltpu.make_async_copy(l_in.at[:, at], l_ref.at[:, at], in_sem.at[1 + 2 * q])

    def r_load(q):
        return pltpu.make_async_copy(r_in.at[q], r_ref.at[q], in_sem.at[2 + 2 * q])

    state_load = pltpu.make_async_copy(state_in, state_ref, in_sem.at[0])
    state_load.start()

    def load(q, carry):
        l_load(q).start()
        r_load(q).start()
        return carry
    lax.fori_loop(0, nq, load, 0)
    s = lax.axis_index("sec")
    k = lax.axis_index("op")
    core = k % 2
    zlo = (k // 2) % 2
    x = k // 4
    nx = no // 4
    d = 1 - 2 * core
    dst, src = s + d, s - d
    has_dst = (dst >= 0) & (dst < ns)
    has_src = (src >= 0) & (src < ns)
    has_up = s < ns - 1
    has_down = s > 0
    charge = charge_ref[0]
    size = sizes_ref[0]
    cells = 1.0 * ns * n * n
    crossed = charge == -d

    barrier = pltpu.get_barrier_semaphore()

    def greet_op(j, carry):
        pl.semaphore_signal(barrier, inc=1, device_id=(s, (k + j) % no), device_id_type=MESH)
        return carry

    def greet_sec(j, carry):
        pl.semaphore_signal(barrier, inc=1, device_id=((s + j) % ns, k), device_id_type=MESH)
        return carry

    lax.fori_loop(1, no, greet_op, 0)
    lax.fori_loop(1, ns, greet_sec, 0)

    def member(dx, dz, dc):
        return ((x + dx) % nx) * 4 + ((zlo + dz) % 2) * 2 + (core + dc) % 2

    def greet_across(j, carry):
        to = ((s + j) % ns, member(0, 1, 0))
        pl.semaphore_signal(barrier, inc=1, device_id=to, device_id_type=MESH)
        return carry

    lax.fori_loop(1, ns, greet_across, 0)

    def op_copy(source, target, send, recv, j):
        return pltpu.make_async_remote_copy(
            src_ref=source, dst_ref=target.at[j], send_sem=send, recv_sem=recv,
            device_id=(s, (k + j) % no), device_id_type=MESH)

    def sec_copy(source, target, send, recv, j):
        return pltpu.make_async_remote_copy(
            src_ref=source, dst_ref=target.at[j], send_sem=send, recv_sem=recv,
            device_id=((s + j) % ns, k), device_id_type=MESH)

    def wait_many(target, send, recv, count):
        whole = target.at[pl.ds(1, count - 1)]
        copy = pltpu.make_async_remote_copy(
            src_ref=whole, dst_ref=whole, send_sem=send, recv_sem=recv,
            device_id=(s, (k + 1) % no), device_id_type=MESH)
        copy.wait_send()
        copy.wait_recv()

    def op_start(which, value):
        op_got[which, 0] = jnp.full((8, 128), value, F32)

        def body(j, carry):
            op_copy(op_got.at[which, 0], op_got.at[which], op_send.at[which], op_recv.at[which], j).start()
            return carry
        lax.fori_loop(1, no, body, 0)

    def op_finish(which):
        wait_many(op_got.at[which], op_send.at[which], op_recv.at[which], no)
        total = jnp.zeros((8, 128), F32)
        for i in range(no):
            total = total + op_got[which, (k + no - i) % no]
        return total

    def sec_start(which, tile):
        sec_got[which, 0] = tile

        def body(j, carry):
            sec_copy(sec_got.at[which, 0], sec_got.at[which], sec_send.at[which], sec_recv.at[which], j).start()
            return carry
        lax.fori_loop(1, ns, body, 0)

    def sec_finish(which):
        wait_many(sec_got.at[which], sec_send.at[which], sec_recv.at[which], ns)
        total = jnp.zeros((8, 128), F32)
        for i in range(ns):
            total = total + sec_got[which, (s + ns - i) % ns]
        return total

    def shifted(source, q):
        return pltpu.make_async_remote_copy(
            src_ref=source.at[q], dst_ref=x_got.at[q], send_sem=x_send.at[q], recv_sem=x_recv.at[q],
            device_id=((dst + ns) % ns, k), device_id_type=MESH)

    half = ns // 2
    at_edge = s == half - 1 + core
    relays = s == (ns - 1) * (1 - core)

    def to_relay(source, q):
        return pltpu.make_async_remote_copy(
            src_ref=source.at[q], dst_ref=x_relay.at[q // 2], send_sem=x_send.at[q], recv_sem=w_recv.at[q // 2],
            device_id=((ns - 1) * (1 - core), member(0, 1, 0)), device_id_type=MESH)

    def from_relay(q):
        return pltpu.make_async_remote_copy(
            src_ref=x_relay.at[q // 2], dst_ref=x_got.at[q], send_sem=w_send.at[q // 2], recv_sem=x_recv.at[q],
            device_id=(half - core, member(0, 1, 0)), device_id_type=MESH)

    def start_shift(source, q):
        by_relay = at_edge & (q % 2 == 1)

        @pl.when(by_relay)
        def _():
            to_relay(source, q).start()

        @pl.when(has_dst & jnp.logical_not(by_relay))
        def _():
            shifted(source, q).start()

    columns = lax.broadcasted_iota(jnp.int32, (share, n), 1) < size
    rows = lax.broadcasted_iota(jnp.int32, (share, n), 0)

    def live(block):
        return columns & (rows + block * share < size)

    def start_block(block):
        return jnp.where(live(block), state_ref[block], 0.0)

    def fill_start(block, total):
        value = start_block(block)
        at = pl.ds(pl.multiple_of(block * share, share), share)
        v_high[at], v_low[at] = split(value)
        return total + jnp.sum((value * value).reshape(share // 8, 8, n), axis=0)

    state_load.wait()
    start_squares = lax.fori_loop(0, no, fill_start, jnp.zeros((8, n), F32))
    start_square = jnp.sum(start_squares)

    @pl.when(jnp.logical_not(has_src))
    def _():
        x_got[...] = jnp.zeros_like(x_got)

    @pl.when(jnp.logical_not(has_up))
    def _():
        t_got[0] = jnp.zeros(t_got.shape[1:], F32)

    @pl.when(jnp.logical_not(has_down))
    def _():
        t_got[1] = jnp.zeros(t_got.shape[1:], F32)


    klass[0] = jnp.full((8, 128), jnp.where(crossed, 1.0, 0.0), F32)

    def x_copy(source, target, send, recv, j):
        return pltpu.make_async_remote_copy(
            src_ref=source, dst_ref=target.at[j], send_sem=send, recv_sem=recv,
            device_id=(s, member(j, 0, 0)), device_id_type=MESH)

    def enter():
        pl.semaphore_wait(barrier, no - 1 + 2 * (ns - 1))
        for j in range(1, nx):
            x_copy(klass.at[0], klass, k_send, k_recv, j).start()

    pair = max(1, 256 // cq)

    def left_products(first):
        def multiply(base, count):
            if first:
                for i in range(count):
                    l_load(base + i).wait()
                    r_load(base + i).wait()
                    at = pl.ds(pl.multiple_of((base + i) * rq, rq), rq)
                    l_high[base + i], l_low[base + i] = split(l_ref[:, at, :].reshape(no * rq, n))
            some = pl.ds(base, count)
            high, low = l_high[some].reshape(count * cq, n), l_low[some].reshape(count * cq, n)
            wide = dot3(high, low, v_high[...], v_low[...], ((1,), (0,)))
            for i in range(count):
                q = base + i
                product = wide[i * cq:(i + 1) * cq]
                x_own[q] = product
                if first:
                    right = r_ref[q]
                    x_sent[q] = jnp.where(charge == d, product, right)
                    p_high[q], p_low[q] = split(jnp.where(crossed, product, right))

        def body(block, carry):
            multiply(block * pair, pair)
            for i in range(pair):
                start_shift(x_sent if first else x_own, block * pair + i)
            return carry

        def single(q, carry):
            multiply(q, 1)
            if first:
                @pl.when(q == 0)
                def _():
                    enter()
            start_shift(x_sent if first else x_own, q)
            return carry
        lax.fori_loop(0, pair, single, 0)
        lax.fori_loop(1, nq // pair, body, 0)

    def t_copy(way, q):
        to = s - 1 if way == 0 else s + 1
        return pltpu.make_async_remote_copy(
            src_ref=t_out.at[way, q], dst_ref=t_got.at[way, q], send_sem=t_send.at[way, q],
            recv_sem=t_recv.at[way, q], device_id=((to + ns) % ns, k), device_id_type=MESH)

    def reduce_x(q):
        wait_many(y_got.at[q], y_send.at[q], y_recv.at[q], nx)
        flags = [jnp.concatenate([klass[j]] * (cq // 128), axis=1)[None] for j in range(nx)]
        for m in range(4):
            parts = [y_out[q, x * 4 + m]] + [y_got[q, j, m] for j in range(1, nx)]
            parts = [part.reshape(share // 8, 8, cq) for part in parts]
            there = [part * flag for part, flag in zip(parts, flags)]
            here = [part - one for part, one in zip(parts, there)]
            z_out[q, m, 0] = sum(here[1:], here[0]).reshape(share, cq)
            z_out[q, m, 1] = sum(there[1:], there[0]).reshape(share, cq)
        for j in range(1, 4):
            z_copy(q, j).start()

    def z_copy(q, j):
        to = (k % 4 + j) % 4
        return pltpu.make_async_remote_copy(
            src_ref=z_out.at[q, to], dst_ref=z_got.at[q, j], send_sem=z_send.at[q], recv_sem=z_recv.at[q],
            device_id=(s, x * 4 + to), device_id_type=MESH)

    def reduce_z(q):
        wait_many(z_got.at[q], z_send.at[q], z_recv.at[q], 4)
        own = z_out[q, k % 4]
        got = [z_got[q, j] for j in range(1, 4)]
        here = (own[0] + got[1][0]) + (got[0][0] + got[2][0])
        same = own[1] + got[1][1]
        other = got[0][1] + got[2][1]
        at = pl.ds(pl.multiple_of(q * rq, rq), rq)
        for p in range(nq):
            sig[at, p * cq:(p + 1) * cq] = here[p * rq:(p + 1) * rq]
        t_out[0, q] = jnp.where(core == 0, same, other)
        t_out[1, q] = jnp.where(core == 0, other, same)

        @pl.when(has_down)
        def _():
            t_copy(0, q).start()

        @pl.when(has_up)
        def _():
            t_copy(1, q).start()

    def right_products(first):
        def body(q, carry):
            @pl.when(relays & (q < nq // 2))
            def _():
                to_relay(x_sent, 2 * q + 1).wait_recv()
                from_relay(2 * q + 1).start()

            @pl.when(has_src)
            def _():
                shifted(x_sent, q).wait_recv()
            use_own = charge == 0 if first else charge != d
            high, low = split(jnp.where(use_own, x_own[q], x_got[q]))
            group = max(1, 256 // cq)
            for start in range(0, nq, group):
                at = pl.ds(start, group)
                wide = dot3(
                    high, low, p_high[at].reshape(group * cq, n), p_low[at].reshape(group * cq, n), ((1,), (1,)))
                for i in range(group):
                    p = start + i
                    block = wide[:, i * cq:(i + 1) * cq]
                    if first:
                        block = jnp.where(crossed, block.T, block)
                    y_out[q, :, p * rq:(p + 1) * rq, :] = block.reshape(no, rq, cq)

            for j in range(1, nx):
                block = y_out.at[q, pl.ds(((x + j) % nx) * 4, 4)]
                x_copy(block, y_got.at[q], y_send.at[q], y_recv.at[q], j).start()

            drain(q, 0)
            return carry

        def drain(q, carry):
            @pl.when((q >= X_LAG) & (q < nq + X_LAG))
            def _():
                reduce_x(q - X_LAG)

            @pl.when(q >= Z_LAG)
            def _():
                reduce_z(q - Z_LAG)
            return carry
        lax.fori_loop(0, nq, body, 0)

        @pl.when(has_dst)
        def _():
            def done(q, carry):
                shifted(x_sent if first else x_own, q).wait_send()
                return carry
            lax.fori_loop(0, nq, done, 0)

        @pl.when(relays)
        def _():
            def passed(i, carry):
                from_relay(2 * i + 1).wait_send()
                return carry
            lax.fori_loop(0, nq // 2, passed, 0)
        if first:
            def keep(q, carry):
                p_high[q], p_low[q] = split(jnp.where(crossed, x_got[q], r_ref[q]))
                return carry
            lax.fori_loop(0, nq, keep, 0)
        lax.fori_loop(nq, nq + Z_LAG, drain, 0)

    def neighbours_in(first):
        def body(q, carry):
            @pl.when(has_up)
            def _():
                t_copy(0, q).wait_recv()

            @pl.when(has_down)
            def _():
                t_copy(1, q).wait_recv()

            @pl.when(has_down)
            def _():
                t_copy(0, q).wait_send()

            @pl.when(has_up)
            def _():
                t_copy(1, q).wait_send()
            return carry
        lax.fori_loop(0, nq, body, 0)
        for q in range(nq):
            both = t_got[0, q] + t_got[1, q]
            if first:
                sig[:, q * cq:(q + 1) * cq] += both
            else:
                for p in range(nq):
                    sig[q * rq:(q + 1) * rq, p * cq:(p + 1) * cq] += both[p * rq:(p + 1) * rq]
        return jnp.where(live(k), sig[...], 0.0)

    left_products(True)
    sec_start(0, jnp.full((8, 128), start_square, F32))
    wait_many(klass, k_send, k_recv, nx)
    right_products(True)
    sigma = neighbours_in(True)

    gathered[k] = sigma

    def g_block(dx, dz, dc, part):
        block = member(nx - dx, dz, dc)
        if part is None:
            return gathered.at[block]
        return gathered.at[block, pl.ds(part * (share // 2), share // 2)]

    def g_copy(dx, dz, dc, to_x, to_z, to_c, part=None):
        block = g_block(dx, dz, dc, part)
        slot = ((dx + to_x) % nx) * 4 + ((dz + to_z) % 2) * 2 + (dc + to_c) % 2
        slot = no + dx if part == 1 else slot
        return pltpu.make_async_remote_copy(
            src_ref=block, dst_ref=block, send_sem=g_send.at[slot], recv_sem=g_recv.at[slot],
            device_id=(s, member(to_x, to_z, to_c)), device_id_type=MESH)

    def g_wait(dx, dz, dc, part=None):
        block = g_block(dx, dz, dc, part)
        slot = no + dx if part == 1 else dx * 4 + dz * 2 + dc
        pltpu.make_async_remote_copy(
            src_ref=block, dst_ref=block, send_sem=g_send.at[slot], recv_sem=g_recv.at[slot],
            device_id=(s, member(0, 0, 1)), device_id_type=MESH).wait_recv()

    sends = []

    def g_start(*arguments):
        copy = g_copy(*arguments)
        copy.start()
        sends.append(copy)

    op_start(0, jnp.sum(sigma * start_block(k)))
    around = [1, nx - 1] + list(range(2, nx - 1))
    g_start(0, 0, 0, 0, 1, 0)
    for step in around:
        g_start(0, 0, 0, step, 0, 0)
    g_start(0, 0, 0, 0, 0, 1)
    sec_start(1, op_finish(0))
    g_wait(0, 1, 0)
    for step in around:
        g_start(0, 1, 0, step, 0, 0, 0)
    g_start(0, 1, 0, 0, 0, 1)
    near, last = around[:2], around[2:]
    for dx in near:
        g_wait(dx, 0, 0)
        g_start(dx, 0, 0, 0, 1, 0, 1)
        g_start(dx, 0, 0, 0, 0, 1)
    start_total = sec_finish(0)
    cross_total = sec_finish(1)
    scale = lax.rsqrt(start_total / cells + epsilon)
    rayleigh_one = cross_total * (scale * scale) / cells
    shift_by = jnp.max(rayleigh_one)

    def residual_block(block):
        return gathered[block] - shift_by * start_block(block)

    def fill_residual(dx, dz, dc):
        block = member(nx - dx, dz, dc)
        value = residual_block(block)
        at = pl.ds(pl.multiple_of(block * share, share), share)
        v_high[at], v_low[at] = split(value)
        rows_sum = jnp.sum((value * value).reshape(share // 8, 8, n), axis=0)
        lanes = [rows_sum[:, i * 128:(i + 1) * 128] for i in range(n // 128)]
        squares[block] = sum(lanes[1:], lanes[0])

    fill_residual(0, 0, 0)
    fill_residual(0, 1, 0)
    for dx in last:
        g_wait(dx, 0, 0)
        g_start(dx, 0, 0, 0, 1, 0, 1)
        g_start(dx, 0, 0, 0, 0, 1)
    for dx in [0] + near:
        g_wait(dx, 0, 1)
        fill_residual(dx, 0, 1)
        if dx:
            fill_residual(dx, 0, 0)
    for dx in around:
        g_wait(dx, 1, 0, 0)
        g_wait(dx, 1, 0, 1)
        g_start(dx, 1, 0, 0, 0, 1)
        fill_residual(dx, 1, 0)
        if dx in last:
            fill_residual(dx, 0, 0)
    for dx in last:
        g_wait(dx, 0, 1)
        fill_residual(dx, 0, 1)
    for dx in [0] + around:
        g_wait(dx, 1, 1)
        fill_residual(dx, 1, 1)

    left_products(False)
    square = jnp.zeros((8, 128), F32)
    for i in range(no):
        square = square + squares[i]
    sec_start(2, jnp.full((8, 128), jnp.sum(square), F32))
    for copy in sends:
        copy.wait_send()
    right_products(False)
    residual_total = sec_finish(2)
    next_tile = scale * lax.rsqrt(residual_total * (scale * scale) / cells + epsilon)
    sigma = neighbours_in(False)
    residual = residual_block(k)
    op_start(1, jnp.sum(sigma * residual))
    nv_ref[0] = residual
    out_sigma_ref[0] = sigma
    sec_start(3, op_finish(1))
    rayleigh_two = sec_finish(3) * (next_tile * next_tile) / cells
    lane = lax.broadcasted_iota(jnp.int32, (8, 128), 1)
    proj_ref[...] = jnp.where(lane == 0, rayleigh_one, jnp.where(lane == 1, rayleigh_two, next_tile))


def on_device(ns, state, left_ops, right_ops, charge, sizes):
    n = state.shape[1]
    no = lax.axis_size("op")
    share = n // no
    nq = CHUNKS
    rq, cq = share // nq, n // nq
    vmem = pltpu.VMEM
    dma = pltpu.SemaphoreType.DMA
    whole = pl.BlockSpec(memory_space=vmem)
    far = pl.BlockSpec(memory_space=pl.ANY)
    small = pl.BlockSpec(memory_space=pltpu.SMEM)
    nv, sigma, proj = pl.pallas_call(
        functools.partial(kernel, nq, ns),
        out_shape=[
            jax.ShapeDtypeStruct((1, share, n), F32),
            jax.ShapeDtypeStruct((1, share, n), F32),
            jax.ShapeDtypeStruct((8, 128), F32),
        ],
        in_specs=[far, far, far, small, small],
        out_specs=[whole, whole, whole],
        scratch_shapes=[
            vmem((no, share, n), F32), vmem((no, share, n), F32), vmem((nq, cq, n), F32),
            vmem((nq, cq, n), BF16), vmem((nq, cq, n), BF16),
            vmem((n, n), BF16), vmem((n, n), BF16),
            vmem((nq, cq, n), BF16), vmem((nq, cq, n), BF16),
            vmem((nq, cq, n), F32), vmem((nq, cq, n), F32), vmem((nq, cq, n), F32),
            vmem((nq // 2, cq, n), F32),
            vmem((nq, no, share, cq), F32), vmem((nq, no // 4, 4, share, cq), F32),
            vmem((nq, 4, 2, share, cq), F32), vmem((nq, 4, 2, share, cq), F32),
            vmem((2, nq, share, cq), F32), vmem((2, nq, share, cq), F32),
            vmem((share, n), F32), vmem((no, share, n), F32),
            vmem((no // 4, 8, 128), F32), vmem((no, 8, 128), F32),
            vmem((2, no, 8, 128), F32), vmem((4, ns, 8, 128), F32),
            dma((nq,)), dma((nq,)), dma((nq // 2,)), dma((nq // 2,)),
            dma((nq,)), dma((nq,)), dma((nq,)), dma((nq,)),
            dma((2, nq)), dma((2, nq)), dma((no + no // 4,)), dma((no + no // 4,)),
            dma, dma, dma((2,)), dma((2,)), dma((4,)), dma((4,)),
            dma((1 + 2 * nq,)),
        ],
        compiler_params=pltpu.CompilerParams(
            collective_id=0, has_side_effects=True, vmem_limit_bytes=60 * 1024 * 1024),
        cost_estimate=pl.CostEstimate(flops=24 * n * n * n, bytes_accessed=12 * n * n, transcendentals=0),
    )(state.reshape(no, share, n), left_ops.reshape(no, share, n), right_ops.reshape(nq, cq, n), charge, sizes)
    next_scale = proj[0, 2]
    return nv * next_scale, sigma * next_scale, proj[0, :2]


def solution(mesh):
    in_specs = (
        P("sec", None, None),
        P("op", "sec", None, None),
        P("op", "sec", None, None),
        P("op"),
        P("sec"),
    )
    out_specs = (P("sec", "op", None), P("sec", "op", None), P())
    return jax.shard_map(
        functools.partial(on_device, mesh.shape["sec"]), mesh=mesh, in_specs=in_specs, out_specs=out_specs,
        check_vma=False)
```

```python
import functools
import jax
import jax.numpy as jnp
from jax import lax
from jax.experimental import pallas as pl
from jax.experimental.pallas import tpu as pltpu
from jax.sharding import PartitionSpec as P

epsilon = 1e-06
CHUNKS = 8
X_LAG = 2
Z_LAG = 4
F32 = jnp.float32
BF16 = jnp.bfloat16
MESH = pl.DeviceIdType.MESH


def split(x):
    high = x.astype(BF16)
    return high, (x - high.astype(F32)).astype(BF16)


def dot3(a_high, a_low, b_high, b_low, contract):
    def one(a, b):
        return lax.dot_general(a, b, (contract, ((), ())), preferred_element_type=F32)
    return one(a_high, b_high) + (one(a_high, b_low) + one(a_low, b_high))


def kernel(
    nq, ns, state_in, l_in, r_in, charge_ref, sizes_ref,
    nv_ref, out_sigma_ref, proj_ref, scale_ref,
    state_ref, l_ref, r_ref, l_high, l_low, v_high, v_low, p_high, p_low, x_own, x_sent, x_got,
    x_relay, y_out, y_got, z_out, z_got, t_out, t_got, sig, gathered, klass, squares, op_got, sec_got,
    x_send, x_recv, w_send, w_recv, y_send, y_recv, z_send, z_recv, t_send, t_recv, g_send, g_recv,
    k_send, k_recv, op_send, op_recv, sec_send, sec_recv,
    in_sem,
):
    no, share, n = state_ref.shape
    rq, cq = share // nq, n // nq

    def l_load(q):
        at = pl.ds(pl.multiple_of(q * rq, rq), rq)
        return pltpu.make_async_copy(l_in.at[:, at], l_ref.at[:, at], in_sem.at[1 + 2 * q])

    def r_load(q):
        return pltpu.make_async_copy(r_in.at[q], r_ref.at[q], in_sem.at[2 + 2 * q])

    state_load = pltpu.make_async_copy(state_in, state_ref, in_sem.at[0])
    state_load.start()

    def load(q, carry):
        l_load(q).start()
        r_load(q).start()
        return carry
    lax.fori_loop(0, nq, load, 0)
    s = lax.axis_index("sec")
    k = lax.axis_index("op")
    core = k % 2
    zlo = (k // 2) % 2
    x = k // 4
    nx = no // 4
    d = 1 - 2 * core
    dst, src = s + d, s - d
    has_dst = (dst >= 0) & (dst < ns)
    has_src = (src >= 0) & (src < ns)
    has_up = s < ns - 1
    has_down = s > 0
    charge = charge_ref[0]
    size = sizes_ref[0]
    cells = 1.0 * ns * n * n
    crossed = charge == -d

    barrier = pltpu.get_barrier_semaphore()

    def greet_op(j, carry):
        pl.semaphore_signal(barrier, inc=1, device_id=(s, (k + j) % no), device_id_type=MESH)
        return carry

    def greet_sec(j, carry):
        pl.semaphore_signal(barrier, inc=1, device_id=((s + j) % ns, k), device_id_type=MESH)
        return carry

    lax.fori_loop(1, no, greet_op, 0)
    lax.fori_loop(1, ns, greet_sec, 0)

    def member(dx, dz, dc):
        return ((x + dx) % nx) * 4 + ((zlo + dz) % 2) * 2 + (core + dc) % 2

    def greet_across(j, carry):
        to = ((s + j) % ns, member(0, 1, 0))
        pl.semaphore_signal(barrier, inc=1, device_id=to, device_id_type=MESH)
        return carry

    lax.fori_loop(1, ns, greet_across, 0)

    def op_copy(source, target, send, recv, j):
        return pltpu.make_async_remote_copy(
            src_ref=source, dst_ref=target.at[j], send_sem=send, recv_sem=recv,
            device_id=(s, (k + j) % no), device_id_type=MESH)

    def sec_copy(source, target, send, recv, j):
        return pltpu.make_async_remote_copy(
            src_ref=source, dst_ref=target.at[j], send_sem=send, recv_sem=recv,
            device_id=((s + j) % ns, k), device_id_type=MESH)

    def wait_many(target, send, recv, count):
        whole = target.at[pl.ds(1, count - 1)]
        copy = pltpu.make_async_remote_copy(
            src_ref=whole, dst_ref=whole, send_sem=send, recv_sem=recv,
            device_id=(s, (k + 1) % no), device_id_type=MESH)
        copy.wait_send()
        copy.wait_recv()

    def op_start(which, value):
        op_got[which, 0] = jnp.full((8, 128), value, F32)

        def body(j, carry):
            op_copy(op_got.at[which, 0], op_got.at[which], op_send.at[which], op_recv.at[which], j).start()
            return carry
        lax.fori_loop(1, no, body, 0)

    def op_finish(which):
        wait_many(op_got.at[which], op_send.at[which], op_recv.at[which], no)
        total = jnp.zeros((8, 128), F32)
        for i in range(no):
            total = total + op_got[which, (k + no - i) % no]
        return total

    def sec_start(which, tile):
        sec_got[which, 0] = tile

        def body(j, carry):
            sec_copy(sec_got.at[which, 0], sec_got.at[which], sec_send.at[which], sec_recv.at[which], j).start()
            return carry
        lax.fori_loop(1, ns, body, 0)

    def sec_finish(which):
        wait_many(sec_got.at[which], sec_send.at[which], sec_recv.at[which], ns)
        total = jnp.zeros((8, 128), F32)
        for i in range(ns):
            total = total + sec_got[which, (s + ns - i) % ns]
        return total

    def shifted(source, q):
        return pltpu.make_async_remote_copy(
            src_ref=source.at[q], dst_ref=x_got.at[q], send_sem=x_send.at[q], recv_sem=x_recv.at[q],
            device_id=((dst + ns) % ns, k), device_id_type=MESH)

    half = ns // 2
    at_edge = s == half - 1 + core
    relays = s == (ns - 1) * (1 - core)

    def to_relay(source, q):
        return pltpu.make_async_remote_copy(
            src_ref=source.at[q], dst_ref=x_relay.at[q // 2], send_sem=x_send.at[q], recv_sem=w_recv.at[q // 2],
            device_id=((ns - 1) * (1 - core), member(0, 1, 0)), device_id_type=MESH)

    def from_relay(q):
        return pltpu.make_async_remote_copy(
            src_ref=x_relay.at[q // 2], dst_ref=x_got.at[q], send_sem=w_send.at[q // 2], recv_sem=x_recv.at[q],
            device_id=(half - core, member(0, 1, 0)), device_id_type=MESH)

    def start_shift(source, q):
        by_relay = at_edge & (q % 2 == 1)

        @pl.when(by_relay)
        def _():
            to_relay(source, q).start()

        @pl.when(has_dst & jnp.logical_not(by_relay))
        def _():
            shifted(source, q).start()

    columns = lax.broadcasted_iota(jnp.int32, (share, n), 1) < size
    rows = lax.broadcasted_iota(jnp.int32, (share, n), 0)

    def live(block):
        return columns & (rows + block * share < size)

    def start_block(block):
        return jnp.where(live(block), state_ref[block], 0.0)

    def fill_start(block, total):
        value = start_block(block)
        at = pl.ds(pl.multiple_of(block * share, share), share)
        v_high[at], v_low[at] = split(value)
        return total + jnp.sum((value * value).reshape(share // 8, 8, n), axis=0)

    state_load.wait()
    start_squares = lax.fori_loop(0, no, fill_start, jnp.zeros((8, n), F32))
    start_square = jnp.sum(start_squares)

    @pl.when(jnp.logical_not(has_src))
    def _():
        x_got[...] = jnp.zeros_like(x_got)

    @pl.when(jnp.logical_not(has_up))
    def _():
        t_got[0] = jnp.zeros(t_got.shape[1:], F32)

    @pl.when(jnp.logical_not(has_down))
    def _():
        t_got[1] = jnp.zeros(t_got.shape[1:], F32)


    klass[0] = jnp.full((8, 128), jnp.where(crossed, 1.0, 0.0), F32)

    def x_copy(source, target, send, recv, j):
        return pltpu.make_async_remote_copy(
            src_ref=source, dst_ref=target.at[j], send_sem=send, recv_sem=recv,
            device_id=(s, member(j, 0, 0)), device_id_type=MESH)

    def enter():
        pl.semaphore_wait(barrier, no - 1 + 2 * (ns - 1))
        for j in range(1, nx):
            x_copy(klass.at[0], klass, k_send, k_recv, j).start()

    pair = max(1, 256 // cq)

    def left_products(first):
        def multiply(base, count):
            if first:
                for i in range(count):
                    l_load(base + i).wait()
                    r_load(base + i).wait()
                    at = pl.ds(pl.multiple_of((base + i) * rq, rq), rq)
                    l_high[base + i], l_low[base + i] = split(l_ref[:, at, :].reshape(no * rq, n))
            some = pl.ds(base, count)
            high, low = l_high[some].reshape(count * cq, n), l_low[some].reshape(count * cq, n)
            wide = dot3(high, low, v_high[...], v_low[...], ((1,), (0,)))
            for i in range(count):
                q = base + i
                product = wide[i * cq:(i + 1) * cq]
                x_own[q] = product
                if first:
                    right = r_ref[q]
                    x_sent[q] = jnp.where(charge == d, product, right)
                    p_high[q], p_low[q] = split(jnp.where(crossed, product, right))

        def body(block, carry):
            multiply(block * pair, pair)
            for i in range(pair):
                start_shift(x_sent if first else x_own, block * pair + i)
            return carry

        def single(q, carry):
            multiply(q, 1)
            if first:
                @pl.when(q == 0)
                def _():
                    enter()
            start_shift(x_sent if first else x_own, q)
            return carry
        lax.fori_loop(0, pair, single, 0)
        lax.fori_loop(1, nq // pair, body, 0)

    def t_copy(way, q):
        to = s - 1 if way == 0 else s + 1
        return pltpu.make_async_remote_copy(
            src_ref=t_out.at[way, q], dst_ref=t_got.at[way, q], send_sem=t_send.at[way, q],
            recv_sem=t_recv.at[way, q], device_id=((to + ns) % ns, k), device_id_type=MESH)

    def reduce_x(q):
        wait_many(y_got.at[q], y_send.at[q], y_recv.at[q], nx)
        flags = [jnp.concatenate([klass[j]] * (cq // 128), axis=1)[None] for j in range(nx)]
        for m in range(4):
            parts = [y_out[q, x * 4 + m]] + [y_got[q, j, m] for j in range(1, nx)]
            parts = [part.reshape(share // 8, 8, cq) for part in parts]
            there = [part * flag for part, flag in zip(parts, flags)]
            here = [part - one for part, one in zip(parts, there)]
            z_out[q, m, 0] = sum(here[1:], here[0]).reshape(share, cq)
            z_out[q, m, 1] = sum(there[1:], there[0]).reshape(share, cq)
        for j in range(1, 4):
            z_copy(q, j).start()

    def z_copy(q, j):
        to = (k % 4 + j) % 4
        return pltpu.make_async_remote_copy(
            src_ref=z_out.at[q, to], dst_ref=z_got.at[q, j], send_sem=z_send.at[q], recv_sem=z_recv.at[q],
            device_id=(s, x * 4 + to), device_id_type=MESH)

    def reduce_z(q):
        wait_many(z_got.at[q], z_send.at[q], z_recv.at[q], 4)
        own = z_out[q, k % 4]
        got = [z_got[q, j] for j in range(1, 4)]
        here = (own[0] + got[1][0]) + (got[0][0] + got[2][0])
        same = own[1] + got[1][1]
        other = got[0][1] + got[2][1]
        at = pl.ds(pl.multiple_of(q * rq, rq), rq)
        for p in range(nq):
            sig[at, p * cq:(p + 1) * cq] = here[p * rq:(p + 1) * rq]
        t_out[0, q] = jnp.where(core == 0, same, other)
        t_out[1, q] = jnp.where(core == 0, other, same)

        @pl.when(has_down)
        def _():
            t_copy(0, q).start()

        @pl.when(has_up)
        def _():
            t_copy(1, q).start()

    def right_products(first):
        def body(q, carry):
            @pl.when(relays & (q < nq // 2))
            def _():
                to_relay(x_sent, 2 * q + 1).wait_recv()
                from_relay(2 * q + 1).start()

            @pl.when(has_src)
            def _():
                shifted(x_sent, q).wait_recv()
            use_own = charge == 0 if first else charge != d
            high, low = split(jnp.where(use_own, x_own[q], x_got[q]))
            group = max(1, 256 // cq)
            for start in range(0, nq, group):
                at = pl.ds(start, group)
                wide = dot3(
                    high, low, p_high[at].reshape(group * cq, n), p_low[at].reshape(group * cq, n), ((1,), (1,)))
                for i in range(group):
                    p = start + i
                    block = wide[:, i * cq:(i + 1) * cq]
                    if first:
                        block = jnp.where(crossed, block.T, block)
                    y_out[q, :, p * rq:(p + 1) * rq, :] = block.reshape(no, rq, cq)

            for j in range(1, nx):
                block = y_out.at[q, pl.ds(((x + j) % nx) * 4, 4)]
                x_copy(block, y_got.at[q], y_send.at[q], y_recv.at[q], j).start()

            drain(q, 0)
            return carry

        def drain(q, carry):
            @pl.when((q >= X_LAG) & (q < nq + X_LAG))
            def _():
                reduce_x(q - X_LAG)

            @pl.when(q >= Z_LAG)
            def _():
                reduce_z(q - Z_LAG)
            return carry
        lax.fori_loop(0, nq, body, 0)

        @pl.when(has_dst)
        def _():
            def done(q, carry):
                shifted(x_sent if first else x_own, q).wait_send()
                return carry
            lax.fori_loop(0, nq, done, 0)

        @pl.when(relays)
        def _():
            def passed(i, carry):
                from_relay(2 * i + 1).wait_send()
                return carry
            lax.fori_loop(0, nq // 2, passed, 0)
        if first:
            def keep(q, carry):
                p_high[q], p_low[q] = split(jnp.where(crossed, x_got[q], r_ref[q]))
                return carry
            lax.fori_loop(0, nq, keep, 0)
        lax.fori_loop(nq, nq + Z_LAG, drain, 0)

    def neighbours_in(first):
        def body(q, carry):
            @pl.when(has_up)
            def _():
                t_copy(0, q).wait_recv()

            @pl.when(has_down)
            def _():
                t_copy(1, q).wait_recv()

            @pl.when(has_down)
            def _():
                t_copy(0, q).wait_send()

            @pl.when(has_up)
            def _():
                t_copy(1, q).wait_send()
            return carry
        lax.fori_loop(0, nq, body, 0)
        for q in range(nq):
            both = t_got[0, q] + t_got[1, q]
            if first:
                sig[:, q * cq:(q + 1) * cq] += both
            else:
                for p in range(nq):
                    sig[q * rq:(q + 1) * rq, p * cq:(p + 1) * cq] += both[p * rq:(p + 1) * rq]
        return jnp.where(live(k), sig[...], 0.0)

    left_products(True)
    sec_start(0, jnp.full((8, 128), start_square, F32))
    wait_many(klass, k_send, k_recv, nx)
    right_products(True)
    sigma = neighbours_in(True)

    gathered[k] = sigma

    def g_block(dx, dz, dc, part):
        block = member(nx - dx, dz, dc)
        if part is None:
            return gathered.at[block]
        return gathered.at[block, pl.ds(part * (share // 2), share // 2)]

    def g_copy(dx, dz, dc, to_x, to_z, to_c, part=None):
        block = g_block(dx, dz, dc, part)
        slot = ((dx + to_x) % nx) * 4 + ((dz + to_z) % 2) * 2 + (dc + to_c) % 2
        slot = no + dx if part == 1 else slot
        return pltpu.make_async_remote_copy(
            src_ref=block, dst_ref=block, send_sem=g_send.at[slot], recv_sem=g_recv.at[slot],
            device_id=(s, member(to_x, to_z, to_c)), device_id_type=MESH)

    def g_wait(dx, dz, dc, part=None):
        block = g_block(dx, dz, dc, part)
        slot = no + dx if part == 1 else dx * 4 + dz * 2 + dc
        pltpu.make_async_remote_copy(
            src_ref=block, dst_ref=block, send_sem=g_send.at[slot], recv_sem=g_recv.at[slot],
            device_id=(s, member(0, 0, 1)), device_id_type=MESH).wait_recv()

    sends = []

    def g_start(*arguments):
        copy = g_copy(*arguments)
        copy.start()
        sends.append(copy)

    op_start(0, jnp.sum(sigma * start_block(k)))
    around = [1, nx - 1] + list(range(2, nx - 1))
    g_start(0, 0, 0, 0, 1, 0)
    for step in around:
        g_start(0, 0, 0, step, 0, 0)
    g_start(0, 0, 0, 0, 0, 1)
    sec_start(1, op_finish(0))
    g_wait(0, 1, 0)
    for step in around:
        g_start(0, 1, 0, step, 0, 0, 0)
    g_start(0, 1, 0, 0, 0, 1)
    near, last = around[:2], around[2:]
    for dx in near:
        g_wait(dx, 0, 0)
        g_start(dx, 0, 0, 0, 1, 0, 1)
        g_start(dx, 0, 0, 0, 0, 1)
    for dx in last:
        g_wait(dx, 0, 0)
        g_start(dx, 0, 0, 0, 1, 0, 1)
        g_start(dx, 0, 0, 0, 0, 1)
    start_total = sec_finish(0)
    cross_total = sec_finish(1)
    scale = lax.rsqrt(start_total / cells + epsilon)
    rayleigh_one = cross_total * (scale * scale) / cells
    shift_by = jnp.max(rayleigh_one)

    def residual_block(block):
        return gathered[block] - shift_by * start_block(block)

    def fill_residual(dx, dz, dc):
        block = member(nx - dx, dz, dc)
        value = residual_block(block)
        at = pl.ds(pl.multiple_of(block * share, share), share)
        v_high[at], v_low[at] = split(value)
        rows_sum = jnp.sum((value * value).reshape(share // 8, 8, n), axis=0)
        lanes = [rows_sum[:, i * 128:(i + 1) * 128] for i in range(n // 128)]
        squares[block] = sum(lanes[1:], lanes[0])

    fill_residual(0, 0, 0)
    fill_residual(0, 1, 0)
    for dx in [0] + near:
        g_wait(dx, 0, 1)
        fill_residual(dx, 0, 1)
        if dx:
            fill_residual(dx, 0, 0)
    for dx in around:
        g_wait(dx, 1, 0, 0)
        g_wait(dx, 1, 0, 1)
        g_start(dx, 1, 0, 0, 0, 1)
        fill_residual(dx, 1, 0)
        if dx in last:
            fill_residual(dx, 0, 0)
    for dx in last:
        g_wait(dx, 0, 1)
        fill_residual(dx, 0, 1)
    for dx in [0] + around:
        g_wait(dx, 1, 1)
        fill_residual(dx, 1, 1)

    left_products(False)
    square = jnp.zeros((8, 128), F32)
    for i in range(no):
        square = square + squares[i]
    sec_start(2, jnp.full((8, 128), jnp.sum(square), F32))
    for copy in sends:
        copy.wait_send()
    right_products(False)
    residual_total = sec_finish(2)
    next_tile = scale * lax.rsqrt(residual_total * (scale * scale) / cells + epsilon)
    sigma = neighbours_in(False)
    residual = residual_block(k)
    op_start(1, jnp.sum(sigma * residual))
    nv_ref[0] = residual
    out_sigma_ref[0] = sigma
    sec_start(3, op_finish(1))
    rayleigh_two = sec_finish(3) * (next_tile * next_tile) / cells
    proj_ref[0] = shift_by
    proj_ref[1] = jnp.max(rayleigh_two)
    scale_ref[0] = jnp.max(next_tile)


def on_device(ns, state, left_ops, right_ops, charge, sizes):
    n = state.shape[1]
    no = lax.axis_size("op")
    share = n // no
    nq = CHUNKS
    rq, cq = share // nq, n // nq
    vmem = pltpu.VMEM
    dma = pltpu.SemaphoreType.DMA
    whole = pl.BlockSpec(memory_space=vmem)
    far = pl.BlockSpec(memory_space=pl.ANY)
    small = pl.BlockSpec(memory_space=pltpu.SMEM)
    nv, sigma, proj, scale = pl.pallas_call(
        functools.partial(kernel, nq, ns),
        out_shape=[
            jax.ShapeDtypeStruct((1, share, n), F32),
            jax.ShapeDtypeStruct((1, share, n), F32),
            jax.ShapeDtypeStruct((2,), F32),
            jax.ShapeDtypeStruct((1,), F32),
        ],
        in_specs=[far, far, far, small, small],
        out_specs=[whole, whole, small, small],
        scratch_shapes=[
            vmem((no, share, n), F32), vmem((no, share, n), F32), vmem((nq, cq, n), F32),
            vmem((nq, cq, n), BF16), vmem((nq, cq, n), BF16),
            vmem((n, n), BF16), vmem((n, n), BF16),
            vmem((nq, cq, n), BF16), vmem((nq, cq, n), BF16),
            vmem((nq, cq, n), F32), vmem((nq, cq, n), F32), vmem((nq, cq, n), F32),
            vmem((nq // 2, cq, n), F32),
            vmem((nq, no, share, cq), F32), vmem((nq, no // 4, 4, share, cq), F32),
            vmem((nq, 4, 2, share, cq), F32), vmem((nq, 4, 2, share, cq), F32),
            vmem((2, nq, share, cq), F32), vmem((2, nq, share, cq), F32),
            vmem((share, n), F32), vmem((no, share, n), F32),
            vmem((no // 4, 8, 128), F32), vmem((no, 8, 128), F32),
            vmem((2, no, 8, 128), F32), vmem((4, ns, 8, 128), F32),
            dma((nq,)), dma((nq,)), dma((nq // 2,)), dma((nq // 2,)),
            dma((nq,)), dma((nq,)), dma((nq,)), dma((nq,)),
            dma((2, nq)), dma((2, nq)), dma((no + no // 4,)), dma((no + no // 4,)),
            dma, dma, dma((2,)), dma((2,)), dma((4,)), dma((4,)),
            dma((1 + 2 * nq,)),
        ],
        compiler_params=pltpu.CompilerParams(
            collective_id=0, has_side_effects=True, vmem_limit_bytes=60 * 1024 * 1024),
        cost_estimate=pl.CostEstimate(flops=24 * n * n * n, bytes_accessed=12 * n * n, transcendentals=0),
    )(state.reshape(no, share, n), left_ops.reshape(no, share, n), right_ops.reshape(nq, cq, n), charge, sizes)
    return nv * scale[0], sigma * scale[0], proj


def solution(mesh):
    in_specs = (
        P("sec", None, None),
        P("op", "sec", None, None),
        P("op", "sec", None, None),
        P("op"),
        P("sec"),
    )
    out_specs = (P("sec", "op", None), P("sec", "op", None), P())
    return jax.shard_map(
        functools.partial(on_device, mesh.shape["sec"]), mesh=mesh, in_specs=in_specs, out_specs=out_specs,
        check_vma=False)
```

```python
import functools
import jax
import jax.numpy as jnp
from jax import lax
from jax.experimental import pallas as pl
from jax.experimental.pallas import tpu as pltpu
from jax.sharding import PartitionSpec as P

epsilon = 1e-06
CHUNKS = 8
X_LAG = 2
Z_LAG = 4
F32 = jnp.float32
BF16 = jnp.bfloat16
MESH = pl.DeviceIdType.MESH


def split(x):
    high = x.astype(BF16)
    return high, (x - high.astype(F32)).astype(BF16)


def dot3(a_high, a_low, b_high, b_low, contract):
    def one(a, b):
        return lax.dot_general(a, b, (contract, ((), ())), preferred_element_type=F32)
    return one(a_high, b_high) + (one(a_high, b_low) + one(a_low, b_high))


def kernel(
    nq, ns, state_in, l_in, r_in, charge_ref, sizes_ref,
    nv_ref, out_sigma_ref, proj_ref, scale_ref,
    state_ref, l_ref, r_ref, l_high, l_low, v_high, v_low, p_high, p_low, x_own, x_sent, x_got,
    x_relay, y_out, y_got, z_out, z_got, t_out, t_got, sig, gathered, klass, squares, op_got, sec_got,
    x_send, x_recv, w_send, w_recv, y_send, y_recv, z_send, z_recv, t_send, t_recv, g_send, g_recv,
    k_send, k_recv, op_send, op_recv, sec_send, sec_recv,
    in_sem,
):
    no, share, n = state_ref.shape
    rq, cq = share // nq, n // nq

    def l_load(q):
        at = pl.ds(pl.multiple_of(q * rq, rq), rq)
        return pltpu.make_async_copy(l_in.at[:, at], l_ref.at[:, at], in_sem.at[1 + 2 * q])

    def r_load(q):
        return pltpu.make_async_copy(r_in.at[q], r_ref.at[q], in_sem.at[2 + 2 * q])

    state_load = pltpu.make_async_copy(state_in, state_ref, in_sem.at[0])
    state_load.start()

    def load(q, carry):
        l_load(q).start()
        r_load(q).start()
        return carry
    lax.fori_loop(0, nq, load, 0)
    s = lax.axis_index("sec")
    k = lax.axis_index("op")
    core = k % 2
    zlo = (k // 2) % 2
    x = k // 4
    nx = no // 4
    d = 1 - 2 * core
    dst, src = s + d, s - d
    has_dst = (dst >= 0) & (dst < ns)
    has_src = (src >= 0) & (src < ns)
    has_up = s < ns - 1
    has_down = s > 0
    charge = charge_ref[0]
    size = sizes_ref[0]
    cells = 1.0 * ns * n * n
    crossed = charge == -d

    barrier = pltpu.get_barrier_semaphore()

    def greet_op(j, carry):
        pl.semaphore_signal(barrier, inc=1, device_id=(s, (k + j) % no), device_id_type=MESH)
        return carry

    def greet_sec(j, carry):
        pl.semaphore_signal(barrier, inc=1, device_id=((s + j) % ns, k), device_id_type=MESH)
        return carry

    lax.fori_loop(1, no, greet_op, 0)
    lax.fori_loop(1, ns, greet_sec, 0)

    def member(dx, dz, dc):
        return ((x + dx) % nx) * 4 + ((zlo + dz) % 2) * 2 + (core + dc) % 2

    def greet_across(j, carry):
        to = ((s + j) % ns, member(0, 1, 0))
        pl.semaphore_signal(barrier, inc=1, device_id=to, device_id_type=MESH)
        return carry

    lax.fori_loop(1, ns, greet_across, 0)

    def op_copy(source, target, send, recv, j):
        return pltpu.make_async_remote_copy(
            src_ref=source, dst_ref=target.at[j], send_sem=send, recv_sem=recv,
            device_id=(s, (k + j) % no), device_id_type=MESH)

    def sec_copy(source, target, send, recv, j):
        return pltpu.make_async_remote_copy(
            src_ref=source, dst_ref=target.at[j], send_sem=send, recv_sem=recv,
            device_id=((s + j) % ns, k), device_id_type=MESH)

    def wait_many(target, send, recv, count):
        whole = target.at[pl.ds(1, count - 1)]
        copy = pltpu.make_async_remote_copy(
            src_ref=whole, dst_ref=whole, send_sem=send, recv_sem=recv,
            device_id=(s, (k + 1) % no), device_id_type=MESH)
        copy.wait_send()
        copy.wait_recv()

    def op_start(which, value):
        op_got[which, 0] = jnp.full((8, 128), value, F32)

        def body(j, carry):
            op_copy(op_got.at[which, 0], op_got.at[which], op_send.at[which], op_recv.at[which], j).start()
            return carry
        lax.fori_loop(1, no, body, 0)

    def op_finish(which):
        wait_many(op_got.at[which], op_send.at[which], op_recv.at[which], no)
        total = jnp.zeros((8, 128), F32)
        for i in range(no):
            total = total + op_got[which, (k + no - i) % no]
        return total

    def sec_start(which, tile):
        sec_got[which, 0] = tile

        def body(j, carry):
            sec_copy(sec_got.at[which, 0], sec_got.at[which], sec_send.at[which], sec_recv.at[which], j).start()
            return carry
        lax.fori_loop(1, ns, body, 0)

    def sec_finish(which):
        wait_many(sec_got.at[which], sec_send.at[which], sec_recv.at[which], ns)
        total = jnp.zeros((8, 128), F32)
        for i in range(ns):
            total = total + sec_got[which, (s + ns - i) % ns]
        return total

    def shifted(source, q):
        return pltpu.make_async_remote_copy(
            src_ref=source.at[q], dst_ref=x_got.at[q], send_sem=x_send.at[q], recv_sem=x_recv.at[q],
            device_id=((dst + ns) % ns, k), device_id_type=MESH)

    half = ns // 2
    at_edge = s == half - 1 + core
    relays = s == (ns - 1) * (1 - core)

    def to_relay(source, q):
        return pltpu.make_async_remote_copy(
            src_ref=source.at[q], dst_ref=x_relay.at[q // 2], send_sem=x_send.at[q], recv_sem=w_recv.at[q // 2],
            device_id=((ns - 1) * (1 - core), member(0, 1, 0)), device_id_type=MESH)

    def from_relay(q):
        return pltpu.make_async_remote_copy(
            src_ref=x_relay.at[q // 2], dst_ref=x_got.at[q], send_sem=w_send.at[q // 2], recv_sem=x_recv.at[q],
            device_id=(half - core, member(0, 1, 0)), device_id_type=MESH)

    def start_shift(source, q):
        by_relay = at_edge & (q % 2 == 1)

        @pl.when(by_relay)
        def _():
            to_relay(source, q).start()

        @pl.when(has_dst & jnp.logical_not(by_relay))
        def _():
            shifted(source, q).start()

    columns = lax.broadcasted_iota(jnp.int32, (share, n), 1) < size
    rows = lax.broadcasted_iota(jnp.int32, (share, n), 0)

    def live(block):
        return columns & (rows + block * share < size)

    def start_block(block):
        return jnp.where(live(block), state_ref[block], 0.0)

    def fill_start(block, total):
        value = start_block(block)
        at = pl.ds(pl.multiple_of(block * share, share), share)
        v_high[at], v_low[at] = split(value)
        return total + jnp.sum((value * value).reshape(share // 8, 8, n), axis=0)

    state_load.wait()
    start_squares = lax.fori_loop(0, no, fill_start, jnp.zeros((8, n), F32))
    start_square = jnp.sum(start_squares)

    @pl.when(jnp.logical_not(has_src))
    def _():
        x_got[...] = jnp.zeros_like(x_got)

    @pl.when(jnp.logical_not(has_up))
    def _():
        t_got[0] = jnp.zeros(t_got.shape[1:], F32)

    @pl.when(jnp.logical_not(has_down))
    def _():
        t_got[1] = jnp.zeros(t_got.shape[1:], F32)


    klass[0] = jnp.full((8, 128), jnp.where(crossed, 1.0, 0.0), F32)

    def x_copy(source, target, send, recv, j):
        return pltpu.make_async_remote_copy(
            src_ref=source, dst_ref=target.at[j], send_sem=send, recv_sem=recv,
            device_id=(s, member(j, 0, 0)), device_id_type=MESH)

    def enter():
        pl.semaphore_wait(barrier, no - 1 + 2 * (ns - 1))
        for j in range(1, nx):
            x_copy(klass.at[0], klass, k_send, k_recv, j).start()

    pair = max(1, 256 // cq)

    def left_products(first):
        def multiply(base, count):
            if first:
                for i in range(count):
                    l_load(base + i).wait()
                    r_load(base + i).wait()
                    at = pl.ds(pl.multiple_of((base + i) * rq, rq), rq)
                    l_high[base + i], l_low[base + i] = split(l_ref[:, at, :].reshape(no * rq, n))
            some = pl.ds(base, count)
            high, low = l_high[some].reshape(count * cq, n), l_low[some].reshape(count * cq, n)
            wide = dot3(high, low, v_high[...], v_low[...], ((1,), (0,)))
            for i in range(count):
                q = base + i
                product = wide[i * cq:(i + 1) * cq]
                x_own[q] = product
                if first:
                    right = r_ref[q]
                    x_sent[q] = jnp.where(charge == d, product, right)
                    p_high[q], p_low[q] = split(jnp.where(crossed, product, right))

        def body(block, carry):
            multiply(block * pair, pair)
            for i in range(pair):
                start_shift(x_sent if first else x_own, block * pair + i)
            return carry

        def single(q, carry):
            multiply(q, 1)
            if first:
                @pl.when(q == 0)
                def _():
                    enter()
            start_shift(x_sent if first else x_own, q)
            return carry
        lax.fori_loop(0, pair, single, 0)
        lax.fori_loop(1, nq // pair, body, 0)

    def t_copy(way, q):
        to = s - 1 if way == 0 else s + 1
        return pltpu.make_async_remote_copy(
            src_ref=t_out.at[way, q], dst_ref=t_got.at[way, q], send_sem=t_send.at[way, q],
            recv_sem=t_recv.at[way, q], device_id=((to + ns) % ns, k), device_id_type=MESH)

    def reduce_x(q):
        wait_many(y_got.at[q], y_send.at[q], y_recv.at[q], nx)
        flags = [jnp.concatenate([klass[j]] * (cq // 128), axis=1)[None] for j in range(nx)]
        for m in range(4):
            parts = [y_out[q, x * 4 + m]] + [y_got[q, j, m] for j in range(1, nx)]
            parts = [part.reshape(share // 8, 8, cq) for part in parts]
            there = [part * flag for part, flag in zip(parts, flags)]
            here = [part - one for part, one in zip(parts, there)]
            z_out[q, m, 0] = sum(here[1:], here[0]).reshape(share, cq)
            z_out[q, m, 1] = sum(there[1:], there[0]).reshape(share, cq)
        for j in range(1, 4):
            z_copy(q, j).start()

    def z_copy(q, j):
        to = (k % 4 + j) % 4
        return pltpu.make_async_remote_copy(
            src_ref=z_out.at[q, to], dst_ref=z_got.at[q, j], send_sem=z_send.at[q], recv_sem=z_recv.at[q],
            device_id=(s, x * 4 + to), device_id_type=MESH)

    def reduce_z(q):
        wait_many(z_got.at[q], z_send.at[q], z_recv.at[q], 4)
        own = z_out[q, k % 4]
        got = [z_got[q, j] for j in range(1, 4)]
        here = (own[0] + got[1][0]) + (got[0][0] + got[2][0])
        same = own[1] + got[1][1]
        other = got[0][1] + got[2][1]
        at = pl.ds(pl.multiple_of(q * rq, rq), rq)
        for p in range(nq):
            sig[at, p * cq:(p + 1) * cq] = here[p * rq:(p + 1) * rq]
        t_out[0, q] = jnp.where(core == 0, same, other)
        t_out[1, q] = jnp.where(core == 0, other, same)

        @pl.when(has_down)
        def _():
            t_copy(0, q).start()

        @pl.when(has_up)
        def _():
            t_copy(1, q).start()

    def right_products(first):
        def body(q, carry):
            @pl.when(relays & (q < nq // 2))
            def _():
                to_relay(x_sent, 2 * q + 1).wait_recv()
                from_relay(2 * q + 1).start()

            @pl.when(has_src)
            def _():
                shifted(x_sent, q).wait_recv()
            use_own = charge == 0 if first else charge != d
            high, low = split(jnp.where(use_own, x_own[q], x_got[q]))
            group = max(1, 256 // cq)
            for start in range(0, nq, group):
                at = pl.ds(start, group)
                wide = dot3(
                    high, low, p_high[at].reshape(group * cq, n), p_low[at].reshape(group * cq, n), ((1,), (1,)))
                for i in range(group):
                    p = start + i
                    block = wide[:, i * cq:(i + 1) * cq]
                    if first:
                        block = jnp.where(crossed, block.T, block)
                    y_out[q, :, p * rq:(p + 1) * rq, :] = block.reshape(no, rq, cq)

            for j in range(1, nx):
                block = y_out.at[q, pl.ds(((x + j) % nx) * 4, 4)]
                x_copy(block, y_got.at[q], y_send.at[q], y_recv.at[q], j).start()

            drain(q, 0)
            return carry

        def drain(q, carry):
            @pl.when((q >= X_LAG) & (q < nq + X_LAG))
            def _():
                reduce_x(q - X_LAG)

            @pl.when(q >= Z_LAG)
            def _():
                reduce_z(q - Z_LAG)
            return carry
        lax.fori_loop(0, nq, body, 0)

        @pl.when(has_dst)
        def _():
            def done(q, carry):
                shifted(x_sent if first else x_own, q).wait_send()
                return carry
            lax.fori_loop(0, nq, done, 0)

        @pl.when(relays)
        def _():
            def passed(i, carry):
                from_relay(2 * i + 1).wait_send()
                return carry
            lax.fori_loop(0, nq // 2, passed, 0)
        if first:
            def keep(q, carry):
                p_high[q], p_low[q] = split(jnp.where(crossed, x_got[q], r_ref[q]))
                return carry
            lax.fori_loop(0, nq, keep, 0)
        lax.fori_loop(nq, nq + X_LAG - 1, drain, 0)
        for q in range(nq + X_LAG - 1 - Z_LAG, nq - 2):
            reduce_z(q)
        reduce_x(nq - 1)
        reduce_z(nq - 2)
        reduce_z(nq - 1)

    def neighbours_in(first):
        def body(q, carry):
            @pl.when(has_up)
            def _():
                t_copy(0, q).wait_recv()

            @pl.when(has_down)
            def _():
                t_copy(1, q).wait_recv()

            @pl.when(has_down)
            def _():
                t_copy(0, q).wait_send()

            @pl.when(has_up)
            def _():
                t_copy(1, q).wait_send()
            return carry
        lax.fori_loop(0, nq, body, 0)
        for q in range(nq):
            both = t_got[0, q] + t_got[1, q]
            if first:
                sig[:, q * cq:(q + 1) * cq] += both
            else:
                for p in range(nq):
                    sig[q * rq:(q + 1) * rq, p * cq:(p + 1) * cq] += both[p * rq:(p + 1) * rq]
        return jnp.where(live(k), sig[...], 0.0)

    left_products(True)
    sec_start(0, jnp.full((8, 128), start_square, F32))
    wait_many(klass, k_send, k_recv, nx)
    right_products(True)
    sigma = neighbours_in(True)

    gathered[k] = sigma

    def g_block(dx, dz, dc, part):
        block = member(nx - dx, dz, dc)
        if part is None:
            return gathered.at[block]
        return gathered.at[block, pl.ds(part * (share // 2), share // 2)]

    def g_copy(dx, dz, dc, to_x, to_z, to_c, part=None):
        block = g_block(dx, dz, dc, part)
        slot = ((dx + to_x) % nx) * 4 + ((dz + to_z) % 2) * 2 + (dc + to_c) % 2
        slot = no + dx if part == 1 else slot
        return pltpu.make_async_remote_copy(
            src_ref=block, dst_ref=block, send_sem=g_send.at[slot], recv_sem=g_recv.at[slot],
            device_id=(s, member(to_x, to_z, to_c)), device_id_type=MESH)

    def g_wait(dx, dz, dc, part=None):
        block = g_block(dx, dz, dc, part)
        slot = no + dx if part == 1 else dx * 4 + dz * 2 + dc
        pltpu.make_async_remote_copy(
            src_ref=block, dst_ref=block, send_sem=g_send.at[slot], recv_sem=g_recv.at[slot],
            device_id=(s, member(0, 0, 1)), device_id_type=MESH).wait_recv()

    sends = []

    def g_start(*arguments):
        copy = g_copy(*arguments)
        copy.start()
        sends.append(copy)

    op_start(0, jnp.sum(sigma * start_block(k)))
    around = [1, nx - 1] + list(range(2, nx - 1))
    g_start(0, 0, 0, 0, 1, 0)
    for step in around:
        g_start(0, 0, 0, step, 0, 0)
    g_start(0, 0, 0, 0, 0, 1)
    sec_start(1, op_finish(0))
    g_wait(0, 1, 0)
    for step in around:
        g_start(0, 1, 0, step, 0, 0, 0)
    g_start(0, 1, 0, 0, 0, 1)
    near, last = around[:2], around[2:]
    for dx in near:
        g_wait(dx, 0, 0)
        g_start(dx, 0, 0, 0, 1, 0, 1)
        g_start(dx, 0, 0, 0, 0, 1)
    for dx in last:
        g_wait(dx, 0, 0)
        g_start(dx, 0, 0, 0, 1, 0, 1)
        g_start(dx, 0, 0, 0, 0, 1)
    start_total = sec_finish(0)
    cross_total = sec_finish(1)
    scale = lax.rsqrt(start_total / cells + epsilon)
    rayleigh_one = cross_total * (scale * scale) / cells
    shift_by = jnp.max(rayleigh_one)

    def residual_block(block):
        return gathered[block] - shift_by * start_block(block)

    def fill_residual(dx, dz, dc):
        block = member(nx - dx, dz, dc)
        value = residual_block(block)
        at = pl.ds(pl.multiple_of(block * share, share), share)
        v_high[at], v_low[at] = split(value)
        rows_sum = jnp.sum((value * value).reshape(share // 8, 8, n), axis=0)
        lanes = [rows_sum[:, i * 128:(i + 1) * 128] for i in range(n // 128)]
        squares[block] = sum(lanes[1:], lanes[0])

    fill_residual(0, 0, 0)
    fill_residual(0, 1, 0)
    for dx in [0] + near:
        g_wait(dx, 0, 1)
        fill_residual(dx, 0, 1)
        if dx:
            fill_residual(dx, 0, 0)
    for dx in around:
        g_wait(dx, 1, 0, 0)
        g_wait(dx, 1, 0, 1)
        g_start(dx, 1, 0, 0, 0, 1)
        fill_residual(dx, 1, 0)
        if dx in last:
            fill_residual(dx, 0, 0)
    for dx in last:
        g_wait(dx, 0, 1)
        fill_residual(dx, 0, 1)
    for dx in [0] + around:
        g_wait(dx, 1, 1)
        fill_residual(dx, 1, 1)

    left_products(False)
    square = jnp.zeros((8, 128), F32)
    for i in range(no):
        square = square + squares[i]
    sec_start(2, jnp.full((8, 128), jnp.sum(square), F32))
    for copy in sends:
        copy.wait_send()
    right_products(False)
    residual_total = sec_finish(2)
    next_tile = scale * lax.rsqrt(residual_total * (scale * scale) / cells + epsilon)
    sigma = neighbours_in(False)
    residual = residual_block(k)
    op_start(1, jnp.sum(sigma * residual))
    nv_ref[0] = residual
    out_sigma_ref[0] = sigma
    sec_start(3, op_finish(1))
    rayleigh_two = sec_finish(3) * (next_tile * next_tile) / cells
    proj_ref[0] = shift_by
    proj_ref[1] = jnp.max(rayleigh_two)
    scale_ref[0] = jnp.max(next_tile)


def on_device(ns, state, left_ops, right_ops, charge, sizes):
    n = state.shape[1]
    no = lax.axis_size("op")
    share = n // no
    nq = CHUNKS
    rq, cq = share // nq, n // nq
    vmem = pltpu.VMEM
    dma = pltpu.SemaphoreType.DMA
    whole = pl.BlockSpec(memory_space=vmem)
    far = pl.BlockSpec(memory_space=pl.ANY)
    small = pl.BlockSpec(memory_space=pltpu.SMEM)
    nv, sigma, proj, scale = pl.pallas_call(
        functools.partial(kernel, nq, ns),
        out_shape=[
            jax.ShapeDtypeStruct((1, share, n), F32),
            jax.ShapeDtypeStruct((1, share, n), F32),
            jax.ShapeDtypeStruct((2,), F32),
            jax.ShapeDtypeStruct((1,), F32),
        ],
        in_specs=[far, far, far, small, small],
        out_specs=[whole, whole, small, small],
        scratch_shapes=[
            vmem((no, share, n), F32), vmem((no, share, n), F32), vmem((nq, cq, n), F32),
            vmem((nq, cq, n), BF16), vmem((nq, cq, n), BF16),
            vmem((n, n), BF16), vmem((n, n), BF16),
            vmem((nq, cq, n), BF16), vmem((nq, cq, n), BF16),
            vmem((nq, cq, n), F32), vmem((nq, cq, n), F32), vmem((nq, cq, n), F32),
            vmem((nq // 2, cq, n), F32),
            vmem((nq, no, share, cq), F32), vmem((nq, no // 4, 4, share, cq), F32),
            vmem((nq, 4, 2, share, cq), F32), vmem((nq, 4, 2, share, cq), F32),
            vmem((2, nq, share, cq), F32), vmem((2, nq, share, cq), F32),
            vmem((share, n), F32), vmem((no, share, n), F32),
            vmem((no // 4, 8, 128), F32), vmem((no, 8, 128), F32),
            vmem((2, no, 8, 128), F32), vmem((4, ns, 8, 128), F32),
            dma((nq,)), dma((nq,)), dma((nq // 2,)), dma((nq // 2,)),
            dma((nq,)), dma((nq,)), dma((nq,)), dma((nq,)),
            dma((2, nq)), dma((2, nq)), dma((no + no // 4,)), dma((no + no // 4,)),
            dma, dma, dma((2,)), dma((2,)), dma((4,)), dma((4,)),
            dma((1 + 2 * nq,)),
        ],
        compiler_params=pltpu.CompilerParams(
            collective_id=0, has_side_effects=True, vmem_limit_bytes=60 * 1024 * 1024),
        cost_estimate=pl.CostEstimate(flops=24 * n * n * n, bytes_accessed=12 * n * n, transcendentals=0),
    )(state.reshape(no, share, n), left_ops.reshape(no, share, n), right_ops.reshape(nq, cq, n), charge, sizes)
    return nv * scale[0], sigma * scale[0], proj


def solution(mesh):
    in_specs = (
        P("sec", None, None),
        P("op", "sec", None, None),
        P("op", "sec", None, None),
        P("op"),
        P("sec"),
    )
    out_specs = (P("sec", "op", None), P("sec", "op", None), P())
    return jax.shard_map(
        functools.partial(on_device, mesh.shape["sec"]), mesh=mesh, in_specs=in_specs, out_specs=out_specs,
        check_vma=False)
```
